256 devices in a mesh: batch: 8 (over z_hi, y), dap: 32 (over z_lo, x, core).
Axes of the slice: x: 4, y: 4, z: 8 (z_hi: 2, z_lo: 4; z = z_hi * 4 + z_lo), core: 2. Of those that a mesh axis runs over, the one named last changes fastest.
Arguments:
- relative_embedding: bfloat16 [4096, 256, 256], P(('batch', 'dap')), parts along dimension 0, may hold values from -6 to 6
- coupling_features: bfloat16 [2048, 256, 128], P(('batch', 'dap')), parts along dimension 0, may hold values from -6 to 6
- relative_variance_multiplier: float32 [256], replicated, may hold values from 0.1 to 1.9
- bilinear_lhs_projector: bfloat16 [256, 32], replicated, may hold values from -0.375 to 0.375
- bilinear_rhs_projector: bfloat16 [256, 32], replicated, may hold values from -0.375 to 0.375
- product_final_matrix: bfloat16 [1024, 128], replicated, may hold values from -4 to 4
- coupling_standard_scale: float32 [128], replicated, may hold values from 0.1 to 1.9
- incoming_edge_matrix: bfloat16 [128, 128], replicated, may hold values from -0.5 to 0.5
- incoming_edge_sigmoid: bfloat16 [128, 128], replicated, may hold values from -0.5 to 0.5
- second_edge_matrix: bfloat16 [128, 128], replicated, may hold values from -0.5 to 0.5
- second_edge_sigmoid: bfloat16 [128, 128], replicated, may hold values from -0.5 to 0.5
- update_sigmoid_matrix: bfloat16 [128, 128], replicated, may hold values from -0.5 to 0.5
- update_final_matrix: bfloat16 [128, 128], replicated, may hold values from -0.5 to 0.5
- cubic_standard_scale: float32 [128], replicated, may hold values from 0.1 to 1.9
Outputs:
- pair_out: bfloat16 [2048, 256, 128], P(('batch', 'dap')), parts along dimension 0
The draws below stay inside these ranges and needn't reach their ends.
There are 8 independent parts, one for each index of `batch`. The reference program is written for one: setup_inputs(seed, part) draws one part's arguments, and reference() takes and returns one part's arrays. A program takes and returns all parts, laid end to end along the dimension named above; an argument that names none is the same for every part. Nothing has to cross between parts.
All inputs are finite; a program needn't handle non-finite values.
Results may differ from the reference program's by a relative error of at most 0.0075.
Values may be sent and summed in bfloat16 or wider, within the bound.
A program may use at most 128 MiB of HBM per device.

```python
import jax
import jax.numpy as jnp
from jax import lax

CLUSTER_WIDTH = 256
PAIR_CH = 128
BILINEAR_HIDDEN = 32
TRI_CH = 128
RELATIVE_DEPTH = 512
PEPTIDE_SPAN = 256


def shard_levels(rng, dims, pieces, smallest, high):
    factor_of = 1.0
    for dim, shards_of in pieces:
        draws = jax.random.uniform(jax.random.fold_in(jax.random.fold_in(rng, 6), dim), (shards_of,), jnp.float32, smallest / len(pieces), high / len(pieces))
        factor_of = factor_of * jnp.repeat(jnp.exp(draws), dims[dim] // shards_of).reshape((-1,) + (1,) * (len(dims) - 1 - dim))
    return factor_of


def scatter_about(key, extent, deviation, reach, pieces=(), dtype=jnp.bfloat16):
    loudness = shard_levels(key, extent, pieces, -0.22, 0.18) if pieces else 1.0
    values = jax.random.normal(key, extent, jnp.float32) * deviation * loudness
    return jnp.minimum(jnp.maximum(values, -reach), reach).astype(dtype)


def setup_inputs(seed: int = 0, part: int = 0) -> dict:
    keys = jax.random.split(jax.random.key(seed), 15)
    own_keys = jax.random.split(jax.random.fold_in(keys[14], part), 15)
    return {
        "relative_embedding": scatter_about(own_keys[0], (RELATIVE_DEPTH, PEPTIDE_SPAN, CLUSTER_WIDTH), 1.0, 6.0, ((0, 32),)),
        "coupling_features": scatter_about(own_keys[1], (PEPTIDE_SPAN, PEPTIDE_SPAN, PAIR_CH), 1.0, 6.0, ((0, 32),)),
        "relative_variance_multiplier": jnp.clip(1.0 + 0.18 * jax.random.normal(keys[2], (CLUSTER_WIDTH,), jnp.float32), 0.1, 1.9),
        "bilinear_lhs_projector": scatter_about(keys[3], (CLUSTER_WIDTH, BILINEAR_HIDDEN), CLUSTER_WIDTH ** -0.5, 0.375),
        "bilinear_rhs_projector": scatter_about(keys[4], (CLUSTER_WIDTH, BILINEAR_HIDDEN), CLUSTER_WIDTH ** -0.5, 0.375),
        "product_final_matrix": scatter_about(keys[5], (BILINEAR_HIDDEN * BILINEAR_HIDDEN, PAIR_CH), (max(1, BILINEAR_HIDDEN * BILINEAR_HIDDEN // RELATIVE_DEPTH)) ** -0.5, 4.0),
        "coupling_standard_scale": jnp.clip(1.0 + 0.18 * jax.random.normal(keys[6], (PAIR_CH,), jnp.float32), 0.1, 1.9),
        "incoming_edge_matrix": scatter_about(keys[7], (PAIR_CH, TRI_CH), PAIR_CH ** -0.5, 0.5),
        "incoming_edge_sigmoid": scatter_about(keys[8], (PAIR_CH, TRI_CH), PAIR_CH ** -0.5, 0.5),
        "second_edge_matrix": scatter_about(keys[9], (PAIR_CH, TRI_CH), PAIR_CH ** -0.5, 0.5),
        "second_edge_sigmoid": scatter_about(keys[10], (PAIR_CH, TRI_CH), PAIR_CH ** -0.5, 0.5),
        "update_sigmoid_matrix": scatter_about(keys[11], (PAIR_CH, PAIR_CH), PAIR_CH ** -0.5, 0.5),
        "update_final_matrix": scatter_about(keys[12], (TRI_CH, PAIR_CH), TRI_CH ** -0.5, 0.5),
        "cubic_standard_scale": jnp.clip(1.0 + 0.18 * jax.random.normal(keys[13], (TRI_CH,), jnp.float32), 0.1, 1.9),
    }


def standardize_features(values, gain):
    mean = lax.optimization_barrier(jnp.mean(values, axis=-1, keepdims=True))
    centred = values - mean
    spread = lax.optimization_barrier(jnp.mean(centred * centred, axis=-1, keepdims=True))
    return centred * lax.rsqrt(spread + 1e-05) * gain.astype(jnp.float32)

def gated_edge(normed, weight, gate):
    opened = jax.nn.sigmoid(jnp.dot(normed, gate, preferred_element_type=jnp.float32))
    return (opened * jnp.dot(normed, weight, preferred_element_type=jnp.float32)).astype(jnp.bfloat16)

def reference(relative_embedding, coupling_features, relative_variance_multiplier, bilinear_lhs_projector, bilinear_rhs_projector, product_final_matrix, coupling_standard_scale, incoming_edge_matrix, incoming_edge_sigmoid, second_edge_matrix, second_edge_sigmoid, update_sigmoid_matrix, update_final_matrix, cubic_standard_scale):
    homolog_standardized = standardize_features(relative_embedding.astype(jnp.float32), relative_variance_multiplier).astype(jnp.bfloat16)
    left_factor = jnp.dot(homolog_standardized, bilinear_lhs_projector, preferred_element_type=jnp.float32).astype(jnp.bfloat16)
    right_factor = jnp.dot(homolog_standardized, bilinear_rhs_projector, preferred_element_type=jnp.float32).astype(jnp.bfloat16)
    outer = jnp.einsum('sic,sjd->ijcd', left_factor.astype(jnp.float32), right_factor.astype(jnp.float32)) * (1.0 / RELATIVE_DEPTH)
    outer = outer.astype(jnp.bfloat16).reshape(PEPTIDE_SPAN, PEPTIDE_SPAN, BILINEAR_HIDDEN * BILINEAR_HIDDEN)
    pair_mid = coupling_features.astype(jnp.float32) + jnp.dot(outer, product_final_matrix, preferred_element_type=jnp.float32)
    pair_norm = standardize_features(pair_mid, coupling_standard_scale).astype(jnp.bfloat16)
    edge_left = gated_edge(pair_norm, incoming_edge_matrix, incoming_edge_sigmoid)
    edge_right = gated_edge(pair_norm, second_edge_matrix, second_edge_sigmoid)
    tri = jnp.einsum('ikc,jkc->ijc', edge_left.astype(jnp.float32), edge_right.astype(jnp.float32))
    tri_norm = standardize_features(tri, cubic_standard_scale).astype(jnp.bfloat16)
    opened = jax.nn.sigmoid(jnp.dot(pair_norm, update_sigmoid_matrix, preferred_element_type=jnp.float32))
    update = opened * jnp.dot(tri_norm, update_final_matrix, preferred_element_type=jnp.float32)
    return (pair_mid + update).astype(jnp.bfloat16)
```

```python
import jax
import jax.numpy as jnp
from jax import lax
from jax.experimental import pallas as pl
from jax.experimental.pallas import tpu as pltpu
from jax.sharding import PartitionSpec as P

MESH = pl.DeviceIdType.MESH
F32 = jnp.float32
BF16 = jnp.bfloat16
CHUNKS = 4
ND = 32 // CHUNKS
NT = (((1,), (1,)), ((), ()))


def remote(src, dst, send_sem, recv_sem, target):
    return pltpu.make_async_remote_copy(
        src_ref=src,
        dst_ref=dst,
        send_sem=send_sem,
        recv_sem=recv_sem,
        device_id={"dap": target},
        device_id_type=MESH,
    )


def column(row):
    return jnp.broadcast_to(row, (128, 128)).T


def norm_rows(v, gain):
    mean = jnp.mean(v, axis=0, keepdims=True)
    centred = v - mean
    spread = jnp.mean(centred * centred, axis=0, keepdims=True)
    return (centred * lax.rsqrt(spread + 1e-05) * gain).astype(BF16)


def kernel(
    msa,
    coup,
    msa_gain,
    w_lhs,
    w_rhs,
    w_final,
    pair_gain,
    w_el,
    g_el,
    w_er,
    g_er,
    g_up,
    w_up,
    tri_gain,
    out,
    s_left,
    s_right,
    l_send,
    l_all,
    l_t,
    r_send,
    r_all,
    outer,
    coup16,
    w2,
    w5,
    wu,
    mid,
    gate,
    s_el,
    s_er,
    e_send,
    e_recv,
    t_send,
    t_recv,
    s_tri,
    o_buf,
    o_got,
    sib_send,
    sib_recv,
    l_ssem,
    l_rsem,
    z_ssem,
    x_ssem,
    f_ssem,
    r_rsem,
    f_rsem,
    e_ssem,
    e_rsem,
    t_ssem,
    t_rsem,
):
    me = lax.axis_index("dap")
    h = me % 2
    q = me // 2
    x = q % 4
    z = q // 4
    sib = 2 * q + (1 - h)

    def dev(zz, xx):
        return 2 * (4 * zz + xx) + h

    barrier = pltpu.get_barrier_semaphore()

    @pl.loop(1, 32)
    def _(k):
        pl.semaphore_signal(
            barrier, inc=1, device_id={"dap": (me + k) % 32}, device_id_type=MESH
        )

    wl4 = jnp.concatenate([w_lhs[...]] * 4, axis=1)
    wrt = w_rhs[...].astype(F32).T.astype(BF16)
    gain = msa_gain[...]

    @pl.loop(0, 16)
    def _(s):
        v = msa[s].astype(F32)
        mean = jnp.mean(v, axis=-1, keepdims=True)
        centred = v - mean
        spread = jnp.mean(centred * centred, axis=-1, keepdims=True)
        normed = (centred * lax.rsqrt(spread + 1e-05) * gain).astype(BF16)
        lp = jnp.dot(normed, wl4, preferred_element_type=F32)
        s_left[pl.ds(s, 256, stride=16), :] = lp
        rp = lax.dot_general(wrt, normed, NT, preferred_element_type=F32)
        s_right[0, pl.ds(s, 32, stride=16), :] = rp[:, :128]
        s_right[1, pl.ds(s, 32, stride=16), :] = rp[:, 128:]

    r_send[...] = s_right[1 - h].reshape(32, 16, 128).astype(BF16)

    pl.semaphore_wait(barrier, 31)

    my16 = pl.ds(pl.multiple_of(me * 16, 16), 16)
    sib_r = remote(r_send, r_all.at[:, my16, :], sib_send.at[0], sib_recv.at[0], sib)
    sib_r.start()
    sib_c = remote(
        coup.at[:, pl.ds(pl.multiple_of((1 - h) * 128, 128), 128), :],
        coup16.at[pl.ds(h * 8, 8)],
        sib_send.at[1],
        sib_recv.at[1],
        sib,
    )
    sib_c.start()
    r_all[:, my16, :] = s_right[h].reshape(32, 16, 128).astype(BF16)

    sib16 = pl.ds(pl.multiple_of(sib * 16, 16), 16)
    remote(r_send, r_all.at[:, sib16, :], sib_send.at[0], sib_recv.at[0], sib).wait_recv()

    def block(c, zz, xx, half=None):
        rows = pl.ds(pl.multiple_of((4 * zz + xx) * 32, 32), 32)
        if half is None:
            return r_all.at[pl.ds(c * ND, ND), rows, :]
        return r_all.at[pl.ds(c * ND + half * (ND // 2), ND // 2), rows, :]

    def z_copy(c, k):
        b = block(c, z, x)
        return remote(b, b, z_ssem.at[c, k], r_rsem.at[c, q], dev((z + k) % 4, x))

    def x_copy(c, zz, d):
        b = block(c, zz, x)
        return remote(
            b, b, x_ssem.at[c, zz, d // 2], r_rsem.at[c, 4 * zz + x], dev(z, (x + d) % 4)
        )

    def f_copy(c, zz, half):
        frm, to = ((x + 3) % 4, (x + 1) % 4) if half == 0 else ((x + 1) % 4, (x + 3) % 4)
        b = block(c, zz, frm, half)
        return remote(b, b, f_ssem.at[c, zz, half], f_rsem.at[c, zz, half], dev(z, to))

    def wait_block(c, zz, xx):
        b = block(c, zz, xx)
        remote(b, b, z_ssem.at[c, 0], r_rsem.at[c, 4 * zz + xx], sib).wait_recv()

    @pl.loop(0, CHUNKS)
    def _(c):
        for k in (1, 2, 3):
            z_copy(c, k).start()
        for d in (1, 3):
            x_copy(c, z, d).start()

    lane = lax.broadcasted_iota(jnp.int32, (4, 16, 128), 2)

    def l_copy(qq):
        return remote(
            l_send.at[qq], l_all.at[q, h], l_ssem.at[qq], l_rsem.at[q], 2 * qq + h
        )

    @pl.loop(0, 16)
    def _(k):
        qq = (q + k) % 16
        v = s_left[pl.ds(pl.multiple_of(qq * 256, 256), 256), :].reshape(4, 4, 16, 128)
        v = jnp.where(
            lane < 32,
            v[:, 0],
            jnp.where(lane < 64, v[:, 1], jnp.where(lane < 96, v[:, 2], v[:, 3])),
        ).astype(BF16)
        for g in range(4):
            l_send[qq, :, g * 128 : (g + 1) * 128] = v[g]

        @pl.when(k > 0)
        def _():
            l_copy(qq).start()

    l_all[q, h] = l_send[q]

    s_tri[0:1024, :] = w_final[...].astype(F32)
    for d in range(32):
        part = s_tri[pl.ds(d, 32, stride=32), :]
        s_tri[1024 + d * 32 : 1024 + (d + 1) * 32, :] = part
    for b in range(8):
        w2[:, b * 128 : (b + 1) * 128] = (
            s_tri[1024 + b * 128 : 1024 + (b + 1) * 128, :].T.astype(BF16)
        )
    for b, ref in enumerate((w_el, g_el, w_er, g_er, g_up)):
        w5[b * 128 : (b + 1) * 128, :] = ref[...].astype(F32).T.astype(BF16)
    wu[...] = w_up[...].astype(F32).T.astype(BF16)

    def l_wait(qq):
        remote(l_send.at[qq], l_all.at[qq, h], l_ssem.at[qq], l_rsem.at[qq], sib).wait_recv()

    def forward(c):
        for k in (1, 2, 3):
            zz = (z + k) % 4
            wait_block(c, zz, x)
            x_copy(c, zz, 1).start()
            x_copy(c, zz, 3).start()
        for k in range(4):
            zz = (z + k) % 4
            wait_block(c, zz, (x + 3) % 4)
            f_copy(c, zz, 0).start()
            wait_block(c, zz, (x + 1) % 4)
            f_copy(c, zz, 1).start()

    def finish(c):
        for k in range(4):
            zz = (z + k) % 4
            for half in (0, 1):
                b = block(c, zz, (x + 2) % 4, half)
                remote(
                    b, b, f_ssem.at[c, zz, half], f_rsem.at[c, zz, half], sib
                ).wait_recv()

        @pl.loop(0, ND // 2)
        def _(p):
            d = c * ND + 2 * p
            rhs = jnp.concatenate([r_all[d], r_all[d + 1]], axis=1)
            o = jnp.dot(l_t[...], rhs, preferred_element_type=F32) * (1.0 / 512)
            o = o.astype(BF16)
            outer[:, d] = o[:, :128].reshape(16, 32, 128)
            outer[:, d + 1] = o[:, 128:].reshape(16, 32, 128)

    forward(0)

    @pl.loop(1, 16)
    def _(k):
        l_wait((q + k) % 16)

    l_fwd = remote(l_all.at[:, h], l_all.at[:, h], sib_send.at[2], sib_recv.at[2], sib)
    l_fwd.start()
    remote(
        l_all.at[:, 1 - h], l_all.at[:, 1 - h], sib_send.at[2], sib_recv.at[2], sib
    ).wait_recv()
    for b in range(4):
        l_t[b * 128 : (b + 1) * 128, :] = (
            l_all[:, :, :, b * 128 : (b + 1) * 128].reshape(512, 128).astype(F32).T.astype(BF16)
        )

    coup16[pl.ds(h * 8, 8)] = coup[:, pl.ds(pl.multiple_of(h * 128, 128), 128), :]

    @pl.loop(1, CHUNKS)
    def _(c):
        forward(c)
        finish(c - 1)

    finish(CHUNKS - 1)

    remote(
        coup.at[:, pl.ds(0, 128), :],
        coup16.at[pl.ds((1 - h) * 8, 8)],
        sib_send.at[1],
        sib_recv.at[1],
        sib,
    ).wait_recv()
    eye = (
        lax.broadcasted_iota(jnp.int32, (128, 128), 0)
        == lax.broadcasted_iota(jnp.int32, (128, 128), 1)
    ).astype(F32).astype(BF16)
    p_gain = column(pair_gain[...])
    t_gain = column(tri_gain[...])

    @pl.loop(0, 8)
    def _(a):
        rhs = jnp.concatenate(
            [outer[2 * a].reshape(1024, 128), outer[2 * a + 1].reshape(1024, 128)], axis=1
        )
        u = jnp.dot(w2[...], rhs, preferred_element_type=F32)
        normed = []
        for e in (0, 1):
            i = 2 * a + e
            m = lax.dot_general(eye, coup16[i], NT, preferred_element_type=F32)
            m = m + u[:, e * 128 : (e + 1) * 128]
            mid[i] = m
            normed.append(norm_rows(m, p_gain))
        y = jnp.dot(w5[...], jnp.concatenate(normed, axis=1), preferred_element_type=F32)
        el = jax.nn.sigmoid(y[128:256]) * y[0:128]
        er = jax.nn.sigmoid(y[384:512]) * y[256:384]
        up = jax.nn.sigmoid(y[512:640])
        for e in (0, 1):
            i = 2 * a + e
            lanes = slice(e * 128, (e + 1) * 128)
            gate[i] = up[:, lanes]
            s_el[pl.ds(i, 128, stride=16), :] = el[:, lanes]
            s_er[pl.ds(i, 128, stride=16), :] = er[:, lanes]

    def e_copy(dst):
        return remote(e_send.at[dst], e_recv.at[me], e_ssem.at[dst], e_rsem.at[me], dst)

    @pl.loop(0, 32)
    def _(k):
        dst = (me + k) % 32
        rows = pl.ds(pl.multiple_of(dst * 64, 64), 64)
        e_send[dst, 0:4] = s_el[rows, :].reshape(4, 16, 128).astype(BF16)
        e_send[dst, 4:8] = s_er[rows, :].reshape(4, 16, 128).astype(BF16)

        @pl.when(k > 0)
        def _():
            e_copy(dst).start()

    e_recv[me] = e_send[me]

    @pl.loop(1, 32)
    def _(k):
        src = (me + k) % 32
        remote(e_send.at[src], e_recv.at[src], e_ssem.at[src], e_rsem.at[src], sib).wait_recv()

    for c in range(4):
        got = e_recv.reshape(16, 2, 8, 16, 128)
        t = None
        for hh in (0, 1):
            lhs = got[:, hh, c].reshape(256, 128)
            rhs = got[:, hh, 4 + c].reshape(256, 128)
            term = lax.dot_general(lhs, rhs, NT, preferred_element_type=F32)
            t = term if t is None else t + term
        t = t.astype(BF16)
        for hh in (0, 1):
            t_send[:, hh, c] = t[:, hh * 128 : (hh + 1) * 128].reshape(16, 16, 128)

    def t_copy(dst):
        return remote(
            t_send.at[dst // 2, dst % 2], t_recv.at[me], t_ssem.at[dst], t_rsem.at[me], dst
        )

    @pl.loop(1, 32)
    def _(k):
        t_copy((me + k) % 32).start()

    t_recv[me] = t_send[q, h]

    @pl.loop(1, 32)
    def _(k):
        src = (me + k) % 32
        remote(
            t_send.at[0, 0], t_recv.at[src], t_ssem.at[src], t_rsem.at[src], sib
        ).wait_recv()

    s_tri[...] = t_recv[...].reshape(2048, 128).astype(F32)

    def result(a):
        normed = [
            norm_rows(s_tri[pl.ds(2 * a + e, 128, stride=16), :], t_gain) for e in (0, 1)
        ]
        y = jnp.dot(wu[...], jnp.concatenate(normed, axis=1), preferred_element_type=F32)
        for e in (0, 1):
            i = 2 * a + e
            r = mid[i] + gate[i] * y[:, e * 128 : (e + 1) * 128]
            o_buf[i] = r.T.astype(BF16)

    @pl.loop(0, 4)
    def _(a):
        result(4 * (1 - h) + a)

    o_copy = remote(
        o_buf.at[pl.ds((1 - h) * 8, 8)], o_got, sib_send.at[3], sib_recv.at[3], sib
    )
    o_copy.start()

    @pl.loop(0, 4)
    def _(a):
        result(4 * h + a)

    out[:, pl.ds(pl.multiple_of(h * 128, 128), 128), :] = o_buf[pl.ds(h * 8, 8)]
    o_copy.wait_recv()
    out[:, pl.ds(pl.multiple_of((1 - h) * 128, 128), 128), :] = o_got[...]

    sib_r.wait_send()
    sib_c.wait_send()
    l_fwd.wait_send()
    o_copy.wait_send()

    @pl.loop(1, 16)
    def _(k):
        l_copy((q + k) % 16).wait_send()

    @pl.loop(0, CHUNKS)
    def _(c):
        for k in (1, 2, 3):
            z_copy(c, k).wait_send()
        for zz in range(4):
            x_copy(c, zz, 1).wait_send()
            x_copy(c, zz, 3).wait_send()
            f_copy(c, zz, 0).wait_send()
            f_copy(c, zz, 1).wait_send()

    @pl.loop(1, 32)
    def _(k):
        e_copy((me + k) % 32).wait_send()
        t_copy((me + k) % 32).wait_send()


def local(
    relative_embedding,
    coupling_features,
    relative_variance_multiplier,
    bilinear_lhs_projector,
    bilinear_rhs_projector,
    product_final_matrix,
    coupling_standard_scale,
    incoming_edge_matrix,
    incoming_edge_sigmoid,
    second_edge_matrix,
    second_edge_sigmoid,
    update_sigmoid_matrix,
    update_final_matrix,
    cubic_standard_scale,
):
    vm = pltpu.VMEM
    dma = pltpu.SemaphoreType.DMA
    return pl.pallas_call(
        kernel,
        out_shape=jax.ShapeDtypeStruct((8, 256, 128), BF16),
        in_specs=[pl.BlockSpec(memory_space=pltpu.VMEM)] * 14,
        out_specs=pl.BlockSpec(memory_space=pltpu.VMEM),
        scratch_shapes=[
            vm((4096, 128), F32),
            vm((2, 512, 128), F32),
            vm((16, 16, 512), BF16),
            vm((16, 2, 16, 512), BF16),
            vm((512, 512), BF16),
            vm((32, 16, 128), BF16),
            vm((32, 512, 128), BF16),
            vm((16, 32, 32, 128), BF16),
            vm((16, 128, 128), BF16),
            vm((128, 1024), BF16),
            vm((640, 128), BF16),
            vm((128, 128), BF16),
            vm((16, 128, 128), F32),
            vm((16, 128, 128), F32),
            vm((2048, 128), F32),
            vm((2048, 128), F32),
            vm((32, 8, 16, 128), BF16),
            vm((32, 8, 16, 128), BF16),
            vm((16, 2, 4, 16, 128), BF16),
            vm((32, 4, 16, 128), BF16),
            vm((2048, 128), F32),
            vm((16, 128, 128), BF16),
            vm((8, 128, 128), BF16),
            dma((4,)),
            dma((4,)),
            dma((16,)),
            dma((16,)),
            dma((CHUNKS, 4)),
            dma((CHUNKS, 4, 2)),
            dma((CHUNKS, 4, 2)),
            dma((CHUNKS, 16)),
            dma((CHUNKS, 4, 2)),
            dma((32,)),
            dma((32,)),
            dma((32,)),
            dma((32,)),
        ],
        compiler_params=pltpu.CompilerParams(
            collective_id=0, has_side_effects=True, vmem_limit_bytes=48 * 1024 * 1024
        ),
    )(
        relative_embedding,
        coupling_features,
        relative_variance_multiplier.reshape(1, -1),
        bilinear_lhs_projector,
        bilinear_rhs_projector,
        product_final_matrix,
        coupling_standard_scale.reshape(1, -1),
        incoming_edge_matrix,
        incoming_edge_sigmoid,
        second_edge_matrix,
        second_edge_sigmoid,
        update_sigmoid_matrix,
        update_final_matrix,
        cubic_standard_scale.reshape(1, -1),
    )


def solution(mesh):
    rows = P(("batch", "dap"), None, None)
    return jax.shard_map(
        local,
        mesh=mesh,
        in_specs=(rows, rows) + (P(),) * 12,
        out_specs=rows,
        check_vma=False,
    )
```

```python
import jax
import jax.numpy as jnp
from jax import lax
from jax.experimental import pallas as pl
from jax.experimental.pallas import tpu as pltpu
from jax.sharding import PartitionSpec as P

MESH = pl.DeviceIdType.MESH
F32 = jnp.float32
BF16 = jnp.bfloat16
CHUNKS = 4
ND = 32 // CHUNKS
NT = (((1,), (1,)), ((), ()))


def remote(src, dst, send_sem, recv_sem, target):
    return pltpu.make_async_remote_copy(
        src_ref=src,
        dst_ref=dst,
        send_sem=send_sem,
        recv_sem=recv_sem,
        device_id={"dap": target},
        device_id_type=MESH,
    )


def column(row):
    return jnp.broadcast_to(row, (128, 128)).T


def norm_rows(v, gain):
    mean = jnp.mean(v, axis=0, keepdims=True)
    centred = v - mean
    spread = jnp.mean(centred * centred, axis=0, keepdims=True)
    return (centred * lax.rsqrt(spread + 1e-05) * gain).astype(BF16)


def kernel(
    msa_h,
    coup_h,
    msa_gain_h,
    w_lhs_h,
    w_rhs_h,
    w_final_h,
    pair_gain_h,
    w_el_h,
    g_el_h,
    w_er_h,
    g_er_h,
    g_up_h,
    w_up_h,
    tri_gain_h,
    out,
    msa,
    msa_gain,
    w_lhs,
    w_rhs,
    w_final,
    gains,
    w_six,
    s_left,
    s_right,
    l_send,
    l_all,
    l_t,
    r_send,
    r_all,
    outer,
    coup16,
    w2,
    w5,
    wu,
    mid,
    gate,
    s_el,
    s_er,
    e_send,
    e_recv,
    t_send,
    t_recv,
    s_tri,
    o_buf,
    o_got,
    in_sem,
    sib_send,
    sib_recv,
    l_ssem,
    l_rsem,
    z_ssem,
    x_ssem,
    f_ssem,
    r_rsem,
    f_rsem,
    e_ssem,
    e_rsem,
    t_ssem,
    t_rsem,
):
    me = lax.axis_index("dap")
    h = me % 2
    q = me // 2
    x = q % 4
    z = q // 4
    sib = 2 * q + (1 - h)

    def dev(zz, xx):
        return 2 * (4 * zz + xx) + h

    def fetch(n, src, dst):
        copy = pltpu.make_async_copy(src, dst, in_sem.at[n])
        copy.start()
        return copy

    first = [
        fetch(0, msa_gain_h, msa_gain),
        fetch(1, w_lhs_h, w_lhs),
        fetch(2, w_rhs_h, w_rhs),
    ]
    parts = [
        fetch(3 + n, msa_h.at[pl.ds(4 * n, 4)], msa.at[pl.ds(4 * n, 4)]) for n in range(4)
    ]
    mine = pl.ds(pl.multiple_of(h * 128, 128), 128)
    other = pl.ds(pl.multiple_of((1 - h) * 128, 128), 128)
    later = [
        fetch(7, w_final_h, w_final),
        fetch(8, pair_gain_h, gains.at[0]),
        fetch(9, tri_gain_h, gains.at[1]),
        fetch(10, coup_h.at[:, mine, :], coup16.at[pl.ds(h * 8, 8)]),
    ]
    for n, ref in enumerate((w_el_h, g_el_h, w_er_h, g_er_h, g_up_h, w_up_h)):
        later.append(fetch(11 + n, ref, w_six.at[n]))

    pending = []
    barrier = pltpu.get_barrier_semaphore()

    @pl.loop(1, 32)
    def _(k):
        pl.semaphore_signal(
            barrier, inc=1, device_id={"dap": (me + k) % 32}, device_id_type=MESH
        )

    for copy in first:
        copy.wait()
    wl4 = jnp.concatenate([w_lhs[...].astype(F32)] * 4, axis=0).T.astype(BF16)
    wrt = w_rhs[...]
    gain = msa_gain[...]

    def project(s):
        v = msa[s].astype(F32)
        mean = jnp.mean(v, axis=-1, keepdims=True)
        centred = v - mean
        spread = jnp.mean(centred * centred, axis=-1, keepdims=True)
        normed = (centred * lax.rsqrt(spread + 1e-05) * gain).astype(BF16)
        lp = jnp.dot(normed, wl4, preferred_element_type=F32)
        s_left[pl.ds(s, 256, stride=16), :] = lp
        rp = lax.dot_general(wrt, normed, NT, preferred_element_type=F32)
        s_right[0, pl.ds(s, 32, stride=16), :] = rp[:, :128]
        s_right[1, pl.ds(s, 32, stride=16), :] = rp[:, 128:]

    for n in range(4):
        parts[n].wait()
        pl.loop(4 * n, 4 * n + 4)(project)

    r_send[...] = s_right[1 - h].reshape(32, 16, 128).astype(BF16)

    pl.semaphore_wait(barrier, 31)

    my16 = pl.ds(pl.multiple_of(me * 16, 16), 16)
    sib_r = remote(r_send, r_all.at[:, my16, :], sib_send.at[0], sib_recv.at[0], sib)
    sib_r.start()
    sib_c = remote(
        coup_h.at[:, other, :],
        coup16.at[pl.ds(h * 8, 8)],
        sib_send.at[1],
        sib_recv.at[1],
        sib,
    )
    sib_c.start()
    pending += [sib_r.wait_send, sib_c.wait_send]
    r_all[:, my16, :] = s_right[h].reshape(32, 16, 128).astype(BF16)

    sib16 = pl.ds(pl.multiple_of(sib * 16, 16), 16)
    remote(r_send, r_all.at[:, sib16, :], sib_send.at[0], sib_recv.at[0], sib).wait_recv()

    def block(c, zz, xx, half=None):
        rows = pl.ds(pl.multiple_of((4 * zz + xx) * 32, 32), 32)
        if half is None:
            return r_all.at[pl.ds(c * ND, ND), rows, :]
        return r_all.at[pl.ds(c * ND + half * (ND // 2), ND // 2), rows, :]

    def z_copy(c, k):
        b = block(c, z, x)
        return remote(b, b, z_ssem.at[c, k], r_rsem.at[c, q], dev((z + k) % 4, x))

    def x_copy(c, zz, d):
        b = block(c, zz, x)
        return remote(
            b, b, x_ssem.at[c, zz, d // 2], r_rsem.at[c, 4 * zz + x], dev(z, (x + d) % 4)
        )

    def f_copy(c, zz, half):
        frm, to = ((x + 3) % 4, (x + 1) % 4) if half == 0 else ((x + 1) % 4, (x + 3) % 4)
        b = block(c, zz, frm, half)
        return remote(b, b, f_ssem.at[c, zz, half], f_rsem.at[c, zz, half], dev(z, to))

    def wait_block(c, zz, xx):
        b = block(c, zz, xx)
        remote(b, b, z_ssem.at[c, 0], r_rsem.at[c, 4 * zz + xx], sib).wait_recv()

    @pl.loop(0, CHUNKS)
    def _(c):
        for k in (1, 2, 3):
            z_copy(c, k).start()
        for d in (1, 3):
            x_copy(c, z, d).start()

    def right_sent():
        @pl.loop(0, CHUNKS)
        def _(c):
            for k in (1, 2, 3):
                z_copy(c, k).wait_send()
            for zz in range(4):
                for n in (0, 1):
                    x_copy(c, zz, 2 * n + 1).wait_send()
                    f_copy(c, zz, n).wait_send()

    pending.append(right_sent)

    lane = lax.broadcasted_iota(jnp.int32, (4, 16, 128), 2)

    def l_copy(qq):
        return remote(
            l_send.at[qq], l_all.at[q, h], l_ssem.at[qq], l_rsem.at[q], 2 * qq + h
        )

    @pl.loop(0, 16)
    def _(k):
        qq = (q + k) % 16
        v = s_left[pl.ds(pl.multiple_of(qq * 256, 256), 256), :].reshape(4, 4, 16, 128)
        v = jnp.where(
            lane < 32,
            v[:, 0],
            jnp.where(lane < 64, v[:, 1], jnp.where(lane < 96, v[:, 2], v[:, 3])),
        ).astype(BF16)
        for g in range(4):
            l_send[qq, :, g * 128 : (g + 1) * 128] = v[g]

        @pl.when(k > 0)
        def _():
            l_copy(qq).start()

    l_all[q, h] = l_send[q]

    def left_sent():
        @pl.loop(1, 16)
        def _(k):
            l_copy((q + k) % 16).wait_send()

    pending.append(left_sent)

    for copy in later:
        copy.wait()
    s_tri[0:1024, :] = w_final[...].astype(F32)
    for d in range(32):
        part = s_tri[pl.ds(d, 32, stride=32), :]
        s_tri[1024 + d * 32 : 1024 + (d + 1) * 32, :] = part
    for b in range(8):
        w2[:, b * 128 : (b + 1) * 128] = (
            s_tri[1024 + b * 128 : 1024 + (b + 1) * 128, :].T.astype(BF16)
        )
    for b in range(5):
        w5[b * 128 : (b + 1) * 128, :] = w_six[b].astype(F32).T.astype(BF16)
    wu[...] = w_six[5].astype(F32).T.astype(BF16)

    def l_wait(qq):
        remote(l_send.at[qq], l_all.at[qq, h], l_ssem.at[qq], l_rsem.at[qq], sib).wait_recv()

    def forward(c):
        for k in (1, 2, 3):
            zz = (z + k) % 4
            wait_block(c, zz, x)
            x_copy(c, zz, 1).start()
            x_copy(c, zz, 3).start()
        for k in range(4):
            zz = (z + k) % 4
            wait_block(c, zz, (x + 3) % 4)
            f_copy(c, zz, 0).start()
            wait_block(c, zz, (x + 1) % 4)
            f_copy(c, zz, 1).start()

    def finish(c):
        for k in range(4):
            zz = (z + k) % 4
            for half in (0, 1):
                b = block(c, zz, (x + 2) % 4, half)
                remote(
                    b, b, f_ssem.at[c, zz, half], f_rsem.at[c, zz, half], sib
                ).wait_recv()

        @pl.loop(0, ND // 2)
        def _(p):
            d = c * ND + 2 * p
            rhs = jnp.concatenate([r_all[d], r_all[d + 1]], axis=1)
            o = jnp.dot(l_t[...], rhs, preferred_element_type=F32) * (1.0 / 512)
            o = o.astype(BF16)
            outer[:, d] = o[:, :128].reshape(16, 32, 128)
            outer[:, d + 1] = o[:, 128:].reshape(16, 32, 128)

    forward(0)

    @pl.loop(1, 16)
    def _(k):
        l_wait((q + k) % 16)

    l_fwd = remote(l_all.at[:, h], l_all.at[:, h], sib_send.at[2], sib_recv.at[2], sib)
    l_fwd.start()
    pending.append(l_fwd.wait_send)
    remote(
        l_all.at[:, 1 - h], l_all.at[:, 1 - h], sib_send.at[2], sib_recv.at[2], sib
    ).wait_recv()
    for b in range(4):
        l_t[b * 128 : (b + 1) * 128, :] = (
            l_all[:, :, :, b * 128 : (b + 1) * 128].reshape(512, 128).astype(F32).T.astype(BF16)
        )

    @pl.loop(1, CHUNKS)
    def _(c):
        forward(c)
        finish(c - 1)

    finish(CHUNKS - 1)

    remote(
        coup_h.at[:, other, :],
        coup16.at[pl.ds((1 - h) * 8, 8)],
        sib_send.at[1],
        sib_recv.at[1],
        sib,
    ).wait_recv()
    eye = (
        lax.broadcasted_iota(jnp.int32, (128, 128), 0)
        == lax.broadcasted_iota(jnp.int32, (128, 128), 1)
    ).astype(F32).astype(BF16)
    p_gain = column(gains[0])
    t_gain = column(gains[1])

    @pl.loop(0, 8)
    def _(a):
        rhs = jnp.concatenate(
            [outer[2 * a].reshape(1024, 128), outer[2 * a + 1].reshape(1024, 128)], axis=1
        )
        u = jnp.dot(w2[...], rhs, preferred_element_type=F32)
        normed = []
        for e in (0, 1):
            i = 2 * a + e
            m = lax.dot_general(eye, coup16[i], NT, preferred_element_type=F32)
            m = m + u[:, e * 128 : (e + 1) * 128]
            mid[i] = m
            normed.append(norm_rows(m, p_gain))
        y = jnp.dot(w5[...], jnp.concatenate(normed, axis=1), preferred_element_type=F32)
        el = jax.nn.sigmoid(y[128:256]) * y[0:128]
        er = jax.nn.sigmoid(y[384:512]) * y[256:384]
        up = jax.nn.sigmoid(y[512:640])
        for e in (0, 1):
            i = 2 * a + e
            lanes = slice(e * 128, (e + 1) * 128)
            gate[i] = up[:, lanes]
            s_el[pl.ds(i, 128, stride=16), :] = el[:, lanes]
            s_er[pl.ds(i, 128, stride=16), :] = er[:, lanes]

    def e_copy(dst):
        return remote(e_send.at[dst], e_recv.at[me], e_ssem.at[dst], e_rsem.at[me], dst)

    @pl.loop(0, 32)
    def _(k):
        dst = (me + k) % 32
        rows = pl.ds(pl.multiple_of(dst * 64, 64), 64)
        e_send[dst, 0:4] = s_el[rows, :].reshape(4, 16, 128).astype(BF16)
        e_send[dst, 4:8] = s_er[rows, :].reshape(4, 16, 128).astype(BF16)

        @pl.when(k > 0)
        def _():
            e_copy(dst).start()

    def edges_sent():
        @pl.loop(1, 32)
        def _(k):
            e_copy((me + k) % 32).wait_send()

    pending.append(edges_sent)
    e_recv[me] = e_send[me]

    @pl.loop(1, 32)
    def _(k):
        src = (me + k) % 32
        remote(e_send.at[src], e_recv.at[src], e_ssem.at[src], e_rsem.at[src], sib).wait_recv()

    for c in range(4):
        got = e_recv.reshape(16, 2, 8, 16, 128)
        t = None
        for hh in (0, 1):
            lhs = got[:, hh, c].reshape(256, 128)
            rhs = got[:, hh, 4 + c].reshape(256, 128)
            term = lax.dot_general(lhs, rhs, NT, preferred_element_type=F32)
            t = term if t is None else t + term
        t = t.astype(BF16)
        for hh in (0, 1):
            t_send[:, hh, c] = t[:, hh * 128 : (hh + 1) * 128].reshape(16, 16, 128)

    def t_copy(dst):
        return remote(
            t_send.at[dst // 2, dst % 2], t_recv.at[me], t_ssem.at[dst], t_rsem.at[me], dst
        )

    @pl.loop(1, 32)
    def _(k):
        t_copy((me + k) % 32).start()

    def tri_sent():
        @pl.loop(1, 32)
        def _(k):
            t_copy((me + k) % 32).wait_send()

    pending.append(tri_sent)
    t_recv[me] = t_send[q, h]

    @pl.loop(1, 32)
    def _(k):
        src = (me + k) % 32
        remote(
            t_send.at[0, 0], t_recv.at[src], t_ssem.at[src], t_rsem.at[src], sib
        ).wait_recv()

    s_tri[...] = t_recv[...].reshape(2048, 128).astype(F32)

    def result(a):
        normed = [
            norm_rows(s_tri[pl.ds(2 * a + e, 128, stride=16), :], t_gain) for e in (0, 1)
        ]
        y = jnp.dot(wu[...], jnp.concatenate(normed, axis=1), preferred_element_type=F32)
        for e in (0, 1):
            i = 2 * a + e
            r = mid[i] + gate[i] * y[:, e * 128 : (e + 1) * 128]
            o_buf[i] = r.T.astype(BF16)

    @pl.loop(0, 4)
    def _(a):
        result(4 * (1 - h) + a)

    o_copy = remote(
        o_buf.at[pl.ds((1 - h) * 8, 8)], o_got, sib_send.at[3], sib_recv.at[3], sib
    )
    o_copy.start()
    pending.append(o_copy.wait_send)

    @pl.loop(0, 4)
    def _(a):
        result(4 * h + a)

    out[:, mine, :] = o_buf[pl.ds(h * 8, 8)]
    o_copy.wait_recv()
    out[:, other, :] = o_got[...]

    for wait in pending:
        wait()


def local(
    relative_embedding,
    coupling_features,
    relative_variance_multiplier,
    bilinear_lhs_projector,
    bilinear_rhs_projector,
    product_final_matrix,
    coupling_standard_scale,
    incoming_edge_matrix,
    incoming_edge_sigmoid,
    second_edge_matrix,
    second_edge_sigmoid,
    update_sigmoid_matrix,
    update_final_matrix,
    cubic_standard_scale,
):
    vm = pltpu.VMEM
    dma = pltpu.SemaphoreType.DMA
    return pl.pallas_call(
        kernel,
        out_shape=jax.ShapeDtypeStruct((8, 256, 128), BF16),
        in_specs=[pl.BlockSpec(memory_space=pl.ANY)] * 14,
        out_specs=pl.BlockSpec(memory_space=pltpu.VMEM),
        scratch_shapes=[
            vm((16, 256, 256), BF16),
            vm((1, 256), F32),
            vm((32, 256), BF16),
            vm((32, 256), BF16),
            vm((1024, 128), BF16),
            vm((2, 1, 128), F32),
            vm((6, 128, 128), BF16),
            vm((4096, 128), F32),
            vm((2, 512, 128), F32),
            vm((16, 16, 512), BF16),
            vm((16, 2, 16, 512), BF16),
            vm((512, 512), BF16),
            vm((32, 16, 128), BF16),
            vm((32, 512, 128), BF16),
            vm((16, 32, 32, 128), BF16),
            vm((16, 128, 128), BF16),
            vm((128, 1024), BF16),
            vm((640, 128), BF16),
            vm((128, 128), BF16),
            vm((16, 128, 128), F32),
            vm((16, 128, 128), F32),
            vm((2048, 128), F32),
            vm((2048, 128), F32),
            vm((32, 8, 16, 128), BF16),
            vm((32, 8, 16, 128), BF16),
            vm((16, 2, 4, 16, 128), BF16),
            vm((32, 4, 16, 128), BF16),
            vm((2048, 128), F32),
            vm((16, 128, 128), BF16),
            vm((8, 128, 128), BF16),
            dma((17,)),
            dma((4,)),
            dma((4,)),
            dma((16,)),
            dma((16,)),
            dma((CHUNKS, 4)),
            dma((CHUNKS, 4, 2)),
            dma((CHUNKS, 4, 2)),
            dma((CHUNKS, 16)),
            dma((CHUNKS, 4, 2)),
            dma((32,)),
            dma((32,)),
            dma((32,)),
            dma((32,)),
        ],
        compiler_params=pltpu.CompilerParams(
            collective_id=0, has_side_effects=True, vmem_limit_bytes=48 * 1024 * 1024
        ),
    )(
        relative_embedding,
        coupling_features,
        relative_variance_multiplier.reshape(1, -1),
        bilinear_lhs_projector.T,
        bilinear_rhs_projector.T,
        product_final_matrix,
        coupling_standard_scale.reshape(1, -1),
        incoming_edge_matrix,
        incoming_edge_sigmoid,
        second_edge_matrix,
        second_edge_sigmoid,
        update_sigmoid_matrix,
        update_final_matrix,
        cubic_standard_scale.reshape(1, -1),
    )


def solution(mesh):
    rows = P(("batch", "dap"), None, None)
    return jax.shard_map(
        local,
        mesh=mesh,
        in_specs=(rows, rows) + (P(),) * 12,
        out_specs=rows,
        check_vma=False,
    )
```

```python
import jax
import jax.numpy as jnp
from jax import lax
from jax.experimental import pallas as pl
from jax.experimental.pallas import tpu as pltpu
from jax.sharding import PartitionSpec as P

MESH = pl.DeviceIdType.MESH
F32 = jnp.float32
BF16 = jnp.bfloat16
CHUNKS = 8
ND = 32 // CHUNKS
NT = (((1,), (1,)), ((), ()))


def remote(src, dst, send_sem, recv_sem, target):
    return pltpu.make_async_remote_copy(
        src_ref=src,
        dst_ref=dst,
        send_sem=send_sem,
        recv_sem=recv_sem,
        device_id={"dap": target},
        device_id_type=MESH,
    )


def column(row):
    return jnp.broadcast_to(row, (128, 128)).T


def norm_rows(v, gain):
    mean = jnp.mean(v, axis=0, keepdims=True)
    centred = v - mean
    spread = jnp.mean(centred * centred, axis=0, keepdims=True)
    return (centred * lax.rsqrt(spread + 1e-05) * gain).astype(BF16)


def kernel(
    msa_h,
    coup_h,
    msa_gain_h,
    w_lhs_h,
    w_rhs_h,
    w_final_h,
    pair_gain_h,
    w_el_h,
    g_el_h,
    w_er_h,
    g_er_h,
    g_up_h,
    w_up_h,
    tri_gain_h,
    out,
    msa,
    msa_gain,
    w_lhs,
    w_rhs,
    w_final,
    gains,
    w_six,
    s_left,
    s_right,
    l_send,
    l_all,
    l_t,
    r_send,
    r_all,
    outer,
    coup16,
    w2,
    w5,
    wu,
    mid,
    gate,
    s_el,
    s_er,
    e_send,
    e_recv,
    t_send,
    t_recv,
    s_tri,
    o_buf,
    o_got,
    in_sem,
    sib_send,
    sib_recv,
    l_ssem,
    l_rsem,
    z_ssem,
    x_ssem,
    f_ssem,
    r_rsem,
    f_rsem,
    e_ssem,
    e_rsem,
    t_ssem,
    t_rsem,
):
    me = lax.axis_index("dap")
    h = me % 2
    q = me // 2
    x = q % 4
    z = q // 4
    sib = 2 * q + (1 - h)

    def dev(zz, xx):
        return 2 * (4 * zz + xx) + h

    def fetch(n, src, dst):
        copy = pltpu.make_async_copy(src, dst, in_sem.at[n])
        copy.start()
        return copy

    first = [
        fetch(0, msa_gain_h, msa_gain),
        fetch(1, w_lhs_h, w_lhs),
        fetch(2, w_rhs_h, w_rhs),
    ]
    parts = [
        fetch(3 + n, msa_h.at[pl.ds(4 * n, 4)], msa.at[pl.ds(4 * n, 4)]) for n in range(4)
    ]
    mine = pl.ds(pl.multiple_of(h * 128, 128), 128)
    other = pl.ds(pl.multiple_of((1 - h) * 128, 128), 128)
    later = [
        fetch(7, w_final_h, w_final),
        fetch(8, pair_gain_h, gains.at[0]),
        fetch(9, tri_gain_h, gains.at[1]),
        fetch(10, coup_h.at[:, mine, :], coup16.at[pl.ds(h * 8, 8)]),
    ]
    for n, ref in enumerate((w_el_h, g_el_h, w_er_h, g_er_h, g_up_h, w_up_h)):
        later.append(fetch(11 + n, ref, w_six.at[n]))

    pending = []
    barrier = pltpu.get_barrier_semaphore()

    @pl.loop(1, 32)
    def _(k):
        pl.semaphore_signal(
            barrier, inc=1, device_id={"dap": (me + k) % 32}, device_id_type=MESH
        )

    for copy in first:
        copy.wait()
    wl4 = jnp.concatenate([w_lhs[...].astype(F32)] * 4, axis=0).T.astype(BF16)
    wrt = w_rhs[...]
    gain = msa_gain[...]

    def project(s):
        v = msa[s].astype(F32)
        mean = jnp.mean(v, axis=-1, keepdims=True)
        centred = v - mean
        spread = jnp.mean(centred * centred, axis=-1, keepdims=True)
        normed = (centred * lax.rsqrt(spread + 1e-05) * gain).astype(BF16)
        lp = jnp.dot(normed, wl4, preferred_element_type=F32)
        s_left[pl.ds(s, 256, stride=16), :] = lp
        rp = lax.dot_general(wrt, normed, NT, preferred_element_type=F32)
        s_right[0, pl.ds(s, 32, stride=16), :] = rp[:, :128]
        s_right[1, pl.ds(s, 32, stride=16), :] = rp[:, 128:]

    for n in range(4):
        parts[n].wait()
        pl.loop(4 * n, 4 * n + 4)(project)

    r_send[...] = s_right[1 - h].reshape(32, 16, 128).astype(BF16)

    pl.semaphore_wait(barrier, 31)

    my16 = pl.ds(pl.multiple_of(me * 16, 16), 16)
    sib_r = remote(r_send, r_all.at[:, my16, :], sib_send.at[0], sib_recv.at[0], sib)
    sib_r.start()
    sib_c = remote(
        coup_h.at[:, other, :],
        coup16.at[pl.ds(h * 8, 8)],
        sib_send.at[1],
        sib_recv.at[1],
        sib,
    )
    sib_c.start()
    pending += [sib_r.wait_send, sib_c.wait_send]
    r_all[:, my16, :] = s_right[h].reshape(32, 16, 128).astype(BF16)

    sib16 = pl.ds(pl.multiple_of(sib * 16, 16), 16)
    remote(r_send, r_all.at[:, sib16, :], sib_send.at[0], sib_recv.at[0], sib).wait_recv()

    def block(c, zz, xx, half=None):
        rows = pl.ds(pl.multiple_of((4 * zz + xx) * 32, 32), 32)
        if half is None:
            return r_all.at[pl.ds(c * ND, ND), rows, :]
        return r_all.at[pl.ds(c * ND + half * (ND // 2), ND // 2), rows, :]

    def z_copy(c, k):
        b = block(c, z, x)
        return remote(b, b, z_ssem.at[c, k], r_rsem.at[c, q], dev((z + k) % 4, x))

    def x_copy(c, zz, d):
        b = block(c, zz, x)
        return remote(
            b, b, x_ssem.at[c, zz, d // 2], r_rsem.at[c, 4 * zz + x], dev(z, (x + d) % 4)
        )

    def f_copy(c, zz, half):
        frm, to = ((x + 3) % 4, (x + 1) % 4) if half == 0 else ((x + 1) % 4, (x + 3) % 4)
        b = block(c, zz, frm, half)
        return remote(b, b, f_ssem.at[c, zz, half], f_rsem.at[c, zz, half], dev(z, to))

    def wait_block(c, zz, xx):
        b = block(c, zz, xx)
        remote(b, b, z_ssem.at[c, 0], r_rsem.at[c, 4 * zz + xx], sib).wait_recv()

    def start(c):
        for k in (1, 2, 3):
            z_copy(c, k).start()
        for d in (1, 3):
            x_copy(c, z, d).start()

    start(0)
    start(1)

    def right_sent():
        @pl.loop(0, CHUNKS)
        def _(c):
            for k in (1, 2, 3):
                z_copy(c, k).wait_send()
            for zz in range(4):
                for n in (0, 1):
                    x_copy(c, zz, 2 * n + 1).wait_send()
                    f_copy(c, zz, n).wait_send()

    pending.append(right_sent)

    lane = lax.broadcasted_iota(jnp.int32, (4, 16, 128), 2)

    def l_copy(qq):
        return remote(
            l_send.at[qq], l_all.at[q, h], l_ssem.at[qq], l_rsem.at[q], 2 * qq + h
        )

    @pl.loop(0, 16)
    def _(k):
        qq = (q + k) % 16
        v = s_left[pl.ds(pl.multiple_of(qq * 256, 256), 256), :].reshape(4, 4, 16, 128)
        v = jnp.where(
            lane < 32,
            v[:, 0],
            jnp.where(lane < 64, v[:, 1], jnp.where(lane < 96, v[:, 2], v[:, 3])),
        ).astype(BF16)
        for g in range(4):
            l_send[qq, :, g * 128 : (g + 1) * 128] = v[g]

        @pl.when(k > 0)
        def _():
            l_copy(qq).start()

    l_all[q, h] = l_send[q]

    def left_sent():
        @pl.loop(1, 16)
        def _(k):
            l_copy((q + k) % 16).wait_send()

    pending.append(left_sent)

    for copy in later:
        copy.wait()
    s_tri[0:1024, :] = w_final[...].astype(F32)
    for d in range(32):
        part = s_tri[pl.ds(d, 32, stride=32), :]
        s_tri[1024 + d * 32 : 1024 + (d + 1) * 32, :] = part
    for b in range(8):
        w2[:, b * 128 : (b + 1) * 128] = (
            s_tri[1024 + b * 128 : 1024 + (b + 1) * 128, :].T.astype(BF16)
        )
    for b in range(5):
        w5[b * 128 : (b + 1) * 128, :] = w_six[b].astype(F32).T.astype(BF16)
    wu[...] = w_six[5].astype(F32).T.astype(BF16)

    def l_wait(qq):
        remote(l_send.at[qq], l_all.at[qq, h], l_ssem.at[qq], l_rsem.at[qq], sib).wait_recv()

    def spread(c, more=True):
        for k in (1, 2, 3):
            zz = (z + k) % 4
            wait_block(c, zz, x)
            x_copy(c, zz, 1).start()
            x_copy(c, zz, 3).start()
        if more:
            start(c + 2)

    def forward(c):
        for k in range(4):
            zz = (z + k) % 4
            wait_block(c, zz, (x + 3) % 4)
            f_copy(c, zz, 0).start()
            wait_block(c, zz, (x + 1) % 4)
            f_copy(c, zz, 1).start()

    def finish(c):
        for k in range(4):
            zz = (z + k) % 4
            for half in (0, 1):
                b = block(c, zz, (x + 2) % 4, half)
                remote(
                    b, b, f_ssem.at[c, zz, half], f_rsem.at[c, zz, half], sib
                ).wait_recv()

        @pl.loop(0, ND // 2)
        def _(p):
            d = c * ND + 2 * p
            rhs = jnp.concatenate([r_all[d], r_all[d + 1]], axis=1)
            o = jnp.dot(l_t[...], rhs, preferred_element_type=F32) * (1.0 / 512)
            o = o.astype(BF16)
            outer[:, d] = o[:, :128].reshape(16, 32, 128)
            outer[:, d + 1] = o[:, 128:].reshape(16, 32, 128)

    spread(0)
    spread(1)
    forward(0)

    @pl.loop(1, 16)
    def _(k):
        l_wait((q + k) % 16)

    l_fwd = remote(l_all.at[:, h], l_all.at[:, h], sib_send.at[2], sib_recv.at[2], sib)
    l_fwd.start()
    pending.append(l_fwd.wait_send)
    remote(
        l_all.at[:, 1 - h], l_all.at[:, 1 - h], sib_send.at[2], sib_recv.at[2], sib
    ).wait_recv()
    for b in range(4):
        l_t[b * 128 : (b + 1) * 128, :] = (
            l_all[:, :, :, b * 128 : (b + 1) * 128].reshape(512, 128).astype(F32).T.astype(BF16)
        )

    @pl.loop(2, CHUNKS - 2)
    def _(c):
        spread(c)
        forward(c - 1)
        finish(c - 2)

    for c in (CHUNKS - 2, CHUNKS - 1):
        spread(c, False)
        forward(c - 1)
        finish(c - 2)
    forward(CHUNKS - 1)
    finish(CHUNKS - 2)
    finish(CHUNKS - 1)

    remote(
        coup_h.at[:, other, :],
        coup16.at[pl.ds((1 - h) * 8, 8)],
        sib_send.at[1],
        sib_recv.at[1],
        sib,
    ).wait_recv()
    eye = (
        lax.broadcasted_iota(jnp.int32, (128, 128), 0)
        == lax.broadcasted_iota(jnp.int32, (128, 128), 1)
    ).astype(F32).astype(BF16)
    p_gain = column(gains[0])
    t_gain = column(gains[1])

    @pl.loop(0, 8)
    def _(a):
        rhs = jnp.concatenate(
            [outer[2 * a].reshape(1024, 128), outer[2 * a + 1].reshape(1024, 128)], axis=1
        )
        u = jnp.dot(w2[...], rhs, preferred_element_type=F32)
        normed = []
        for e in (0, 1):
            i = 2 * a + e
            m = lax.dot_general(eye, coup16[i], NT, preferred_element_type=F32)
            m = m + u[:, e * 128 : (e + 1) * 128]
            mid[i] = m
            normed.append(norm_rows(m, p_gain))
        y = jnp.dot(w5[...], jnp.concatenate(normed, axis=1), preferred_element_type=F32)
        el = jax.nn.sigmoid(y[128:256]) * y[0:128]
        er = jax.nn.sigmoid(y[384:512]) * y[256:384]
        up = jax.nn.sigmoid(y[512:640])
        for e in (0, 1):
            i = 2 * a + e
            lanes = slice(e * 128, (e + 1) * 128)
            gate[i] = up[:, lanes]
            s_el[pl.ds(i, 128, stride=16), :] = el[:, lanes]
            s_er[pl.ds(i, 128, stride=16), :] = er[:, lanes]

    zh = me // 16
    m_own = me % 16

    def e_near(g, m):
        return remote(
            e_send.at[m, g], e_recv.at[me, g], e_ssem.at[g, m], e_rsem.at[g, me], zh * 16 + m
        )

    def e_far(g, m):
        return remote(
            e_send.at[m, g, pl.ds(4, 4)],
            e_recv.at[me, g, pl.ds(4, 4)],
            e_ssem.at[g, 16 + m],
            e_rsem.at[g, me],
            (1 - zh) * 16 + m,
        )

    for g in (0, 1):

        @pl.loop(0, 16)
        def _(k):
            m = (m_own + k) % 16
            rows = pl.ds(pl.multiple_of(m * 128 + g * 64, 64), 64)
            e_send[m, g, 0:4] = s_el[rows, :].reshape(4, 16, 128).astype(BF16)
            e_send[m, g, 4:8] = s_er[rows, :].reshape(4, 16, 128).astype(BF16)
            e_far(g, m).start()

            @pl.when(k > 0)
            def _():
                e_near(g, m).start()

        e_recv[me, g] = e_send[m_own, g]

    def edges_sent():
        for g in (0, 1):

            @pl.loop(0, 16)
            def _(k):
                m = (m_own + k) % 16
                e_far(g, m).wait_send()

                @pl.when(k > 0)
                def _():
                    e_near(g, m).wait_send()

    pending.append(edges_sent)

    def t_copy(g, m):
        return remote(
            t_send.at[m // 2, m % 2, g],
            t_recv.at[m_own, g],
            t_ssem.at[g, m],
            t_rsem.at[g, m_own],
            zh * 16 + m,
        )

    got = e_recv.reshape(2, 8, 2, 2, 8, 16, 128)
    for g in (0, 1):

        @pl.loop(0, 16)
        def _(k):
            m = (m_own + k) % 16
            far = (1 - zh) * 16 + m
            near = zh * 16 + m
            remote(
                e_send.at[m, g, pl.ds(4, 4)],
                e_recv.at[far, g, pl.ds(4, 4)],
                e_ssem.at[g, m],
                e_rsem.at[g, far],
                sib,
            ).wait_recv()

            @pl.when(k > 0)
            def _():
                remote(
                    e_send.at[m, g], e_recv.at[near, g], e_ssem.at[g, m], e_rsem.at[g, near], sib
                ).wait_recv()

        for c in range(4):
            t = None
            for hh in (0, 1):
                lhs = got[zh, :, hh, g, c].reshape(128, 128)
                rhs = got[:, :, hh, g, 4 + c].reshape(256, 128)
                term = lax.dot_general(lhs, rhs, NT, preferred_element_type=F32)
                t = term if t is None else t + term
            t = t.astype(BF16)
            for hh in (0, 1):
                t_send[:, hh, g, c] = t[:, hh * 128 : (hh + 1) * 128].reshape(8, 16, 128)

        @pl.loop(1, 16)
        def _(k):
            t_copy(g, (m_own + k) % 16).start()

        t_recv[m_own, g] = t_send[m_own // 2, h, g]

    def tri_sent():
        for g in (0, 1):

            @pl.loop(1, 16)
            def _(k):
                t_copy(g, (m_own + k) % 16).wait_send()

    pending.append(tri_sent)
    for g in (0, 1):

        @pl.loop(1, 16)
        def _(k):
            m = (m_own + k) % 16
            remote(
                t_send.at[0, 0, g], t_recv.at[m, g], t_ssem.at[g, m], t_rsem.at[g, m], sib
            ).wait_recv()

    s_tri[...] = t_recv[...].reshape(2048, 128).astype(F32)

    def result(a):
        normed = [
            norm_rows(s_tri[pl.ds(2 * a + e, 128, stride=16), :], t_gain) for e in (0, 1)
        ]
        y = jnp.dot(wu[...], jnp.concatenate(normed, axis=1), preferred_element_type=F32)
        for e in (0, 1):
            i = 2 * a + e
            r = mid[i] + gate[i] * y[:, e * 128 : (e + 1) * 128]
            o_buf[i] = r.T.astype(BF16)

    @pl.loop(0, 4)
    def _(a):
        result(4 * (1 - h) + a)

    o_copy = remote(
        o_buf.at[pl.ds((1 - h) * 8, 8)], o_got, sib_send.at[3], sib_recv.at[3], sib
    )
    o_copy.start()
    pending.append(o_copy.wait_send)

    @pl.loop(0, 4)
    def _(a):
        result(4 * h + a)

    out[:, mine, :] = o_buf[pl.ds(h * 8, 8)]
    o_copy.wait_recv()
    out[:, other, :] = o_got[...]

    for wait in pending:
        wait()


def local(
    relative_embedding,
    coupling_features,
    relative_variance_multiplier,
    bilinear_lhs_projector,
    bilinear_rhs_projector,
    product_final_matrix,
    coupling_standard_scale,
    incoming_edge_matrix,
    incoming_edge_sigmoid,
    second_edge_matrix,
    second_edge_sigmoid,
    update_sigmoid_matrix,
    update_final_matrix,
    cubic_standard_scale,
):
    vm = pltpu.VMEM
    dma = pltpu.SemaphoreType.DMA
    return pl.pallas_call(
        kernel,
        out_shape=jax.ShapeDtypeStruct((8, 256, 128), BF16),
        in_specs=[pl.BlockSpec(memory_space=pl.ANY)] * 14,
        out_specs=pl.BlockSpec(memory_space=pltpu.VMEM),
        scratch_shapes=[
            vm((16, 256, 256), BF16),
            vm((1, 256), F32),
            vm((32, 256), BF16),
            vm((32, 256), BF16),
            vm((1024, 128), BF16),
            vm((2, 1, 128), F32),
            vm((6, 128, 128), BF16),
            vm((4096, 128), F32),
            vm((2, 512, 128), F32),
            vm((16, 16, 512), BF16),
            vm((16, 2, 16, 512), BF16),
            vm((512, 512), BF16),
            vm((32, 16, 128), BF16),
            vm((32, 512, 128), BF16),
            vm((16, 32, 32, 128), BF16),
            vm((16, 128, 128), BF16),
            vm((128, 1024), BF16),
            vm((640, 128), BF16),
            vm((128, 128), BF16),
            vm((16, 128, 128), F32),
            vm((16, 128, 128), F32),
            vm((2048, 128), F32),
            vm((2048, 128), F32),
            vm((16, 2, 8, 16, 128), BF16),
            vm((32, 2, 8, 16, 128), BF16),
            vm((8, 2, 2, 4, 16, 128), BF16),
            vm((16, 2, 4, 16, 128), BF16),
            vm((2048, 128), F32),
            vm((16, 128, 128), BF16),
            vm((8, 128, 128), BF16),
            dma((17,)),
            dma((4,)),
            dma((4,)),
            dma((16,)),
            dma((16,)),
            dma((CHUNKS, 4)),
            dma((CHUNKS, 4, 2)),
            dma((CHUNKS, 4, 2)),
            dma((CHUNKS, 16)),
            dma((CHUNKS, 4, 2)),
            dma((2, 32)),
            dma((2, 32)),
            dma((2, 16)),
            dma((2, 16)),
        ],
        compiler_params=pltpu.CompilerParams(
            collective_id=0, has_side_effects=True, vmem_limit_bytes=60 * 1024 * 1024
        ),
    )(
        relative_embedding,
        coupling_features,
        relative_variance_multiplier.reshape(1, -1),
        bilinear_lhs_projector.T,
        bilinear_rhs_projector.T,
        product_final_matrix,
        coupling_standard_scale.reshape(1, -1),
        incoming_edge_matrix,
        incoming_edge_sigmoid,
        second_edge_matrix,
        second_edge_sigmoid,
        update_sigmoid_matrix,
        update_final_matrix,
        cubic_standard_scale.reshape(1, -1),
    )


def solution(mesh):
    rows = P(("batch", "dap"), None, None)
    return jax.shard_map(
        local,
        mesh=mesh,
        in_specs=(rows, rows) + (P(),) * 12,
        out_specs=rows,
        check_vma=False,
    )
```

```python
import jax
import jax.numpy as jnp
from jax import lax
from jax.experimental import pallas as pl
from jax.experimental.pallas import tpu as pltpu
from jax.sharding import PartitionSpec as P

MESH = pl.DeviceIdType.MESH
F32 = jnp.float32
BF16 = jnp.bfloat16
CHUNKS = 8
ND = 32 // CHUNKS
NT = (((1,), (1,)), ((), ()))


def remote(src, dst, send_sem, recv_sem, target):
    return pltpu.make_async_remote_copy(
        src_ref=src,
        dst_ref=dst,
        send_sem=send_sem,
        recv_sem=recv_sem,
        device_id={"dap": target},
        device_id_type=MESH,
    )


def column(row):
    return jnp.broadcast_to(row, (128, 128)).T


def norm_rows(v, gain):
    mean = jnp.mean(v, axis=0, keepdims=True)
    centred = v - mean
    spread = jnp.mean(centred * centred, axis=0, keepdims=True)
    return (centred * lax.rsqrt(spread + 1e-05) * gain).astype(BF16)


def kernel(
    msa_h,
    coup_h,
    msa_gain_h,
    w_lhs_h,
    w_rhs_h,
    w_final_h,
    pair_gain_h,
    w_el_h,
    g_el_h,
    w_er_h,
    g_er_h,
    g_up_h,
    w_up_h,
    tri_gain_h,
    out,
    msa,
    msa_gain,
    w_lhs,
    w_rhs,
    w_final,
    gains,
    w_six,
    s_left,
    s_right,
    l_send,
    l_all,
    l_t,
    r_send,
    r_all,
    outer,
    coup16,
    w2,
    w5,
    wu,
    mid,
    gate,
    normed,
    s_el,
    s_er,
    e_send,
    e_recv,
    t_send,
    t_recv,
    s_tri,
    o_buf,
    o_got,
    in_sem,
    sib_send,
    sib_recv,
    l_ssem,
    l_rsem,
    z_ssem,
    x_ssem,
    f_ssem,
    z_rsem,
    x_rsem,
    f_rsem,
    e_ssem,
    e_rsem,
    t_ssem,
    t_rsem,
):
    me = lax.axis_index("dap")
    h = me % 2
    q = me // 2
    x = q % 4
    z = q // 4
    sib = 2 * q + (1 - h)
    pos = 4 * x + z

    def dev(zz, xx):
        return 2 * (4 * zz + xx) + h

    def fetch(n, src, dst):
        copy = pltpu.make_async_copy(src, dst, in_sem.at[n])
        copy.start()
        return copy

    first = [
        fetch(0, msa_gain_h, msa_gain),
        fetch(1, w_lhs_h, w_lhs),
        fetch(2, w_rhs_h, w_rhs),
    ]
    parts = [
        fetch(3 + n, msa_h.at[pl.ds(4 * n, 4)], msa.at[pl.ds(4 * n, 4)]) for n in range(4)
    ]
    mine = pl.ds(pl.multiple_of(h * 128, 128), 128)
    other = pl.ds(pl.multiple_of((1 - h) * 128, 128), 128)
    later = [
        fetch(7, w_final_h, w_final),
        fetch(8, pair_gain_h, gains.at[0]),
        fetch(9, tri_gain_h, gains.at[1]),
        fetch(10, coup_h.at[:, mine, :], coup16.at[pl.ds(h * 8, 8)]),
    ]
    for n, ref in enumerate((w_el_h, g_el_h, w_er_h, g_er_h, g_up_h, w_up_h)):
        fetch(11, ref, w_six.at[n])
    later.append(pltpu.make_async_copy(w_six, w_six, in_sem.at[11]))

    pending = []
    barrier = pltpu.get_barrier_semaphore()

    @pl.loop(1, 32)
    def _(k):
        pl.semaphore_signal(
            barrier, inc=1, device_id={"dap": (me + k) % 32}, device_id_type=MESH
        )

    for copy in first:
        copy.wait()
    wl4 = jnp.concatenate([w_lhs[...].astype(F32)] * 4, axis=0).T.astype(BF16)
    wrt = w_rhs[...]
    gain = msa_gain[...]

    def project(s):
        v = msa[s].astype(F32)
        mean = jnp.mean(v, axis=-1, keepdims=True)
        centred = v - mean
        spread = jnp.mean(centred * centred, axis=-1, keepdims=True)
        normed = (centred * lax.rsqrt(spread + 1e-05) * gain).astype(BF16)
        lp = jnp.dot(normed, wl4, preferred_element_type=F32)
        s_left[pl.ds(s, 256, stride=16), :] = lp
        rp = lax.dot_general(wrt, normed, NT, preferred_element_type=F32)
        s_right[0, pl.ds(s, 32, stride=16), :] = rp[:, :128]
        s_right[1, pl.ds(s, 32, stride=16), :] = rp[:, 128:]

    for n in range(4):
        parts[n].wait()
        pl.loop(4 * n, 4 * n + 4)(project)

    r_send[...] = s_right[1 - h].reshape(32, 16, 128).astype(BF16)

    pl.semaphore_wait(barrier, 31)

    my16 = pl.ds(pl.multiple_of((2 * pos + h) * 16, 16), 16)
    sib_r = remote(r_send, r_all.at[:, my16, :], sib_send.at[0], sib_recv.at[0], sib)
    sib_r.start()
    sib_c = remote(
        coup_h.at[:, other, :],
        coup16.at[pl.ds(h * 8, 8)],
        sib_send.at[1],
        sib_recv.at[1],
        sib,
    )
    sib_c.start()
    pending += [sib_r.wait_send, sib_c.wait_send]
    r_all[:, my16, :] = s_right[h].reshape(32, 16, 128).astype(BF16)

    sib16 = pl.ds(pl.multiple_of((2 * pos + 1 - h) * 16, 16), 16)
    remote(r_send, r_all.at[:, sib16, :], sib_send.at[0], sib_recv.at[0], sib).wait_recv()

    def block(c, zz, xx):
        rows = pl.ds(pl.multiple_of((4 * xx + zz) * 32, 32), 32)
        return r_all.at[pl.ds(c * ND, ND), rows, :]

    def blocks(c, xx, half=None):
        rows = pl.ds(pl.multiple_of(xx * 128, 128), 128)
        if half is None:
            return r_all.at[pl.ds(c * ND, ND), rows, :]
        return r_all.at[pl.ds(c * ND + half * (ND // 2), ND // 2), rows, :]

    def z_copy(c, k):
        b = block(c, z, x)
        return remote(b, b, z_ssem, z_rsem.at[c], dev((z + k) % 4, x))

    def x_copy(c, zz, n):
        b = block(c, zz, x)
        return remote(b, b, x_ssem, x_rsem.at[c, n], dev(z, (x + 1 + 2 * n) % 4))

    def f_copy(c, n):
        b = blocks(c, (x + 3 - 2 * n) % 4, n)
        return remote(b, b, f_ssem, f_rsem.at[c, n], dev(z, (x + 1 + 2 * n) % 4))

    def z_wait(c):
        three = r_all.at[pl.ds(c * ND, ND), pl.ds(0, 96), :]
        remote(three, three, z_ssem, z_rsem.at[c], sib).wait_recv()

    def x_wait(c, n):
        b = blocks(c, (x + 3 - 2 * n) % 4)
        remote(b, b, x_ssem, x_rsem.at[c, n], sib).wait_recv()

    def f_wait(c, n):
        b = blocks(c, (x + 2) % 4, n)
        remote(b, b, f_ssem, f_rsem.at[c, n], sib).wait_recv()

    def z_start(c):
        for k in (1, 2, 3):
            z_copy(c, k).start()

    def sent(ref, sem):
        pending.append(remote(ref, ref, sem, sib_recv.at[0], sib).wait_send)

    z_start(0)

    @pl.loop(0, CHUNKS)
    def _(c):
        for n in (0, 1):
            x_copy(c, z, n).start()

    z_start(1)
    sent(r_all.at[pl.ds(0, 3 * CHUNKS), pl.ds(0, 32 * ND), :], z_ssem)
    sent(r_all.at[pl.ds(0, 16)], x_ssem)
    sent(r_all.at[pl.ds(0, 8)], f_ssem)

    lane = lax.broadcasted_iota(jnp.int32, (4, 16, 128), 2)

    def l_copy(qq):
        return remote(
            l_send.at[qq], l_all.at[pos, h], l_ssem, l_rsem, 2 * qq + h
        )

    @pl.loop(0, 16)
    def _(k):
        qq = (q + k) % 16
        v = s_left[pl.ds(pl.multiple_of(qq * 256, 256), 256), :].reshape(4, 4, 16, 128)
        v = jnp.where(
            lane < 32,
            v[:, 0],
            jnp.where(lane < 64, v[:, 1], jnp.where(lane < 96, v[:, 2], v[:, 3])),
        ).astype(BF16)
        for g in range(4):
            l_send[qq, :, g * 128 : (g + 1) * 128] = v[g]

        @pl.when(k > 0)
        def _():
            l_copy(qq).start()

    l_all[pos, h] = l_send[q]

    sent(l_all.at[pl.ds(0, 15), 0], l_ssem)

    def spread(c):
        z_wait(c)
        for k in (1, 2, 3):
            for n in (0, 1):
                x_copy(c, (z + k) % 4, n).start()
        if c + 2 < CHUNKS:
            z_start(c + 2)

    def forward(c):
        for n in (0, 1):
            x_wait(c, n)
            f_copy(c, n).start()

    def finish(c):
        for n in (0, 1):
            f_wait(c, n)

        for p in range(ND // 2):
            d = c * ND + 2 * p
            rhs = jnp.concatenate([r_all[d], r_all[d + 1]], axis=1)
            o = jnp.dot(l_t[...], rhs, preferred_element_type=F32) * (1.0 / 512)
            o = o.astype(BF16)
            outer[:, 2 * p] = o[:, :128].reshape(16, 32, 128)
            outer[:, 2 * p + 1] = o[:, 128:].reshape(16, 32, 128)

        @pl.loop(0, 8)
        def _(a):
            rhs = jnp.concatenate(
                [outer[2 * a].reshape(128, 128), outer[2 * a + 1].reshape(128, 128)], axis=1
            )
            u = jnp.dot(w2[c], rhs, preferred_element_type=F32)
            mid[2 * a] += u[:, :128]
            mid[2 * a + 1] += u[:, 128:]

    spread(0)
    spread(1)

    for copy in later:
        copy.wait()
    s_tri[0:1024, :] = w_final[...].astype(F32)
    for d in range(32):
        part = s_tri[pl.ds(d, 32, stride=32), :]
        s_tri[1024 + d * 32 : 1024 + (d + 1) * 32, :] = part
    for b in range(8):
        w2[b] = s_tri[1024 + b * 128 : 1024 + (b + 1) * 128, :].T.astype(BF16)
    for b in range(4):
        t = w_six[b].astype(F32).T.astype(BF16)
        w5[0, b * 64 : (b + 1) * 64, :] = t[:64]
        w5[1, b * 64 : (b + 1) * 64, :] = t[64:]
    for b in range(2):
        wu[b] = w_six[4 + b].astype(F32).T.astype(BF16)
    p_gain = column(gains[0])
    t_gain = column(gains[1])

    spread(2)
    forward(0)

    remote(
        coup_h.at[:, other, :],
        coup16.at[pl.ds((1 - h) * 8, 8)],
        sib_send.at[1],
        sib_recv.at[1],
        sib,
    ).wait_recv()
    eye = (
        lax.broadcasted_iota(jnp.int32, (128, 128), 0)
        == lax.broadcasted_iota(jnp.int32, (128, 128), 1)
    ).astype(F32).astype(BF16)

    @pl.loop(0, 16)
    def _(i):
        mid[i] = lax.dot_general(eye, coup16[i], NT, preferred_element_type=F32)

    forward(1)
    remote(
        l_all.at[pl.ds(0, 15), h], l_all.at[pl.ds(0, 15), h], l_ssem, l_rsem, sib
    ).wait_recv()
    l_fwd = remote(l_all.at[:, h], l_all.at[:, h], sib_send.at[2], sib_recv.at[2], sib)
    l_fwd.start()
    pending.append(l_fwd.wait_send)
    spread(3)
    remote(
        l_all.at[:, 1 - h], l_all.at[:, 1 - h], sib_send.at[2], sib_recv.at[2], sib
    ).wait_recv()
    for b in range(4):
        l_t[b * 128 : (b + 1) * 128, :] = (
            l_all[:, :, :, b * 128 : (b + 1) * 128].reshape(512, 128).astype(F32).T.astype(BF16)
        )

    finish(0)
    forward(2)
    finish(1)
    for c in range(4, CHUNKS):
        spread(c)
        forward(c - 1)
        finish(c - 2)
    forward(CHUNKS - 1)
    finish(CHUNKS - 2)
    finish(CHUNKS - 1)


    zh = me // 16
    m_own = me % 16

    def e_near(g, m):
        return remote(e_send.at[m, g], e_recv.at[me, g], e_ssem, e_rsem.at[g], zh * 16 + m)

    def e_far(g, m):
        four = pl.ds(4, 4)
        return remote(
            e_send.at[m, g, four],
            e_recv.at[me, g, four],
            e_ssem,
            e_rsem.at[g],
            (1 - zh) * 16 + m,
        )

    def edges(g, a):
        y = jnp.dot(w5[g], normed[a], preferred_element_type=F32)
        el = jax.nn.sigmoid(y[64:128]) * y[0:64]
        er = jax.nn.sigmoid(y[192:256]) * y[128:192]
        for e in (0, 1):
            rows = pl.ds(2 * a + e, 64, stride=16)
            s_el[rows, :] = el[:, e * 128 : (e + 1) * 128]
            s_er[rows, :] = er[:, e * 128 : (e + 1) * 128]

    def edges_send(g):
        @pl.loop(0, 16)
        def _(k):
            m = (m_own + k) % 16
            rows = pl.ds(pl.multiple_of(m * 64, 64), 64)
            e_send[m, g, 0:4] = s_el[rows, :].reshape(4, 16, 128).astype(BF16)
            e_send[m, g, 4:8] = s_er[rows, :].reshape(4, 16, 128).astype(BF16)
            e_far(g, m).start()

            @pl.when(k > 0)
            def _():
                e_near(g, m).start()

        e_recv[me, g] = e_send[m_own, g]

    @pl.loop(0, 8)
    def _(a):
        normed[a, :, 0:128] = norm_rows(mid[2 * a], p_gain)
        normed[a, :, 128:256] = norm_rows(mid[2 * a + 1], p_gain)
        edges(0, a)

    edges_send(0)

    @pl.loop(0, 8)
    def _(a):
        edges(1, a)

    edges_send(1)
    sent(r_all.at[pl.ds(0, 23), pl.ds(0, 256), :], e_ssem)

    @pl.loop(0, 8)
    def _(a):
        y = jax.nn.sigmoid(jnp.dot(wu[0], normed[a], preferred_element_type=F32))
        gate[2 * a] = y[:, :128]
        gate[2 * a + 1] = y[:, 128:]

    def t_copy(g, m):
        return remote(
            t_send.at[m // 2, m % 2, g], t_recv.at[m_own, g], t_ssem, t_rsem.at[g], zh * 16 + m
        )

    got = e_recv.reshape(2, 8, 2, 2, 8, 16, 128)
    for g in (0, 1):
        every = r_all.at[pl.ds(0, 23), pl.ds(0, 128), :]
        remote(every, every, e_ssem, e_rsem.at[g], sib).wait_recv()

        for c in range(4):
            t = None
            for hh in (0, 1):
                lhs = got[zh, :, hh, g, c].reshape(128, 128)
                rhs = got[:, :, hh, g, 4 + c].reshape(256, 128)
                term = lax.dot_general(lhs, rhs, NT, preferred_element_type=F32)
                t = term if t is None else t + term
            t = t.astype(BF16)
            for hh in (0, 1):
                t_send[:, hh, g, c] = t[:, hh * 128 : (hh + 1) * 128].reshape(8, 16, 128)

        @pl.loop(1, 16)
        def _(k):
            t_copy(g, (m_own + k) % 16).start()

        t_recv[m_own, g] = t_send[m_own // 2, h, g]

    sent(r_all.at[pl.ds(0, 15), pl.ds(0, 128), :], t_ssem)
    for g in (0, 1):
        fifteen = t_recv.at[pl.ds(0, 15), g]
        remote(fifteen, fifteen, t_ssem, t_rsem.at[g], sib).wait_recv()
        s_tri[g * 1024 : (g + 1) * 1024, :] = t_recv[:, g].reshape(1024, 128).astype(F32)


    def result(a):
        rows = [
            norm_rows(s_tri[pl.ds(2 * a + e, 128, stride=16), :], t_gain) for e in (0, 1)
        ]
        y = jnp.dot(wu[1], jnp.concatenate(rows, axis=1), preferred_element_type=F32)
        for e in (0, 1):
            i = 2 * a + e
            r = mid[i] + gate[i] * y[:, e * 128 : (e + 1) * 128]
            o_buf[i] = r.T.astype(BF16)

    @pl.loop(0, 4)
    def _(a):
        result(4 * (1 - h) + a)

    o_copy = remote(
        o_buf.at[pl.ds((1 - h) * 8, 8)], o_got, sib_send.at[3], sib_recv.at[3], sib
    )
    o_copy.start()
    pending.append(o_copy.wait_send)

    @pl.loop(0, 4)
    def _(a):
        result(4 * h + a)

    out[:, mine, :] = o_buf[pl.ds(h * 8, 8)]
    o_copy.wait_recv()
    out[:, other, :] = o_got[...]

    for wait in pending:
        wait()


def local(
    relative_embedding,
    coupling_features,
    relative_variance_multiplier,
    bilinear_lhs_projector,
    bilinear_rhs_projector,
    product_final_matrix,
    coupling_standard_scale,
    incoming_edge_matrix,
    incoming_edge_sigmoid,
    second_edge_matrix,
    second_edge_sigmoid,
    update_sigmoid_matrix,
    update_final_matrix,
    cubic_standard_scale,
):
    vm = pltpu.VMEM
    dma = pltpu.SemaphoreType.DMA
    return pl.pallas_call(
        kernel,
        out_shape=jax.ShapeDtypeStruct((8, 256, 128), BF16),
        in_specs=[pl.BlockSpec(memory_space=pl.ANY)] * 14,
        out_specs=pl.BlockSpec(memory_space=pltpu.VMEM),
        scratch_shapes=[
            vm((16, 256, 256), BF16),
            vm((1, 256), F32),
            vm((32, 256), BF16),
            vm((32, 256), BF16),
            vm((1024, 128), BF16),
            vm((2, 1, 128), F32),
            vm((6, 128, 128), BF16),
            vm((4096, 128), F32),
            vm((2, 512, 128), F32),
            vm((16, 16, 512), BF16),
            vm((16, 2, 16, 512), BF16),
            vm((512, 512), BF16),
            vm((32, 16, 128), BF16),
            vm((32, 512, 128), BF16),
            vm((16, ND, 32, 128), BF16),
            vm((16, 128, 128), BF16),
            vm((CHUNKS, 128, 128), BF16),
            vm((2, 256, 128), BF16),
            vm((2, 128, 128), BF16),
            vm((16, 128, 128), F32),
            vm((16, 128, 128), F32),
            vm((8, 128, 256), BF16),
            vm((1024, 128), F32),
            vm((1024, 128), F32),
            vm((16, 2, 8, 16, 128), BF16),
            vm((32, 2, 8, 16, 128), BF16),
            vm((8, 2, 2, 4, 16, 128), BF16),
            vm((16, 2, 4, 16, 128), BF16),
            vm((2048, 128), F32),
            vm((16, 128, 128), BF16),
            vm((8, 128, 128), BF16),
            dma((12,)),
            dma((4,)),
            dma((4,)),
            dma,
            dma,
            dma,
            dma,
            dma,
            dma((CHUNKS,)),
            dma((CHUNKS, 2)),
            dma((CHUNKS, 2)),
            dma,
            dma((2,)),
            dma,
            dma((2,)),
        ],
        compiler_params=pltpu.CompilerParams(
            collective_id=0, has_side_effects=True, vmem_limit_bytes=60 * 1024 * 1024
        ),
    )(
        relative_embedding,
        coupling_features,
        relative_variance_multiplier.reshape(1, -1),
        bilinear_lhs_projector.T,
        bilinear_rhs_projector.T,
        product_final_matrix,
        coupling_standard_scale.reshape(1, -1),
        incoming_edge_matrix,
        incoming_edge_sigmoid,
        second_edge_matrix,
        second_edge_sigmoid,
        update_sigmoid_matrix,
        update_final_matrix,
        cubic_standard_scale.reshape(1, -1),
    )


def solution(mesh):
    rows = P(("batch", "dap"), None, None)
    return jax.shard_map(
        local,
        mesh=mesh,
        in_specs=(rows, rows) + (P(),) * 12,
        out_specs=rows,
        check_vma=False,
    )
```

```python
import functools

import jax
import jax.numpy as jnp
from jax import lax
from jax.experimental import pallas as pl
from jax.experimental.pallas import tpu as pltpu
from jax.sharding import PartitionSpec as P

MESH = pl.DeviceIdType.MESH
F32 = jnp.float32
BF16 = jnp.bfloat16
CHUNKS = 8
ND = 32 // CHUNKS
GROUPS = (2, 4, 2)
NT = (((1,), (1,)), ((), ()))


def remote(src, dst, send_sem, recv_sem, target):
    return pltpu.make_async_remote_copy(
        src_ref=src,
        dst_ref=dst,
        send_sem=send_sem,
        recv_sem=recv_sem,
        device_id={"dap": target},
        device_id_type=MESH,
    )


def column(row):
    return jnp.broadcast_to(row, (128, 128)).T


def norm_rows(v, gain):
    mean = jnp.mean(v, axis=0, keepdims=True)
    centred = v - mean
    spread = jnp.mean(centred * centred, axis=0, keepdims=True)
    return (centred * lax.rsqrt(spread + 1e-05) * gain).astype(BF16)


def kernel(
    msa_h,
    coup_h,
    msa_gain_h,
    w_lhs_h,
    w_rhs_h,
    w_final_h,
    pair_gain_h,
    w_el_h,
    g_el_h,
    w_er_h,
    g_er_h,
    g_up_h,
    w_up_h,
    tri_gain_h,
    out,
    msa,
    msa_gain,
    w_lhs,
    w_rhs,
    w_final,
    gains,
    w_six,
    s_left,
    s_right,
    l_send,
    l_stage,
    l_all,
    l_t,
    r_send,
    r_all,
    outer,
    coup16,
    w2,
    w5,
    wu,
    mid,
    gate,
    normed,
    s_el,
    s_er,
    e_send,
    e_recv,
    t_send,
    t_recv,
    s_tri,
    o_buf,
    o_got,
    in_sem,
    sib_send,
    sib_recv,
    l_ssem,
    l_rsem,
    z_ssem,
    x_ssem,
    f_ssem,
    z_rsem,
    x_rsem,
    f_rsem,
    e_ssem,
    e_rsem,
    t_ssem,
    t_rsem,
):
    me = lax.axis_index("dap")
    h = me % 2
    q = me // 2
    x = q % 4
    z = q // 4
    sib = 2 * q + (1 - h)
    pos = 4 * x + z

    def dev(zz, xx):
        return 2 * (4 * zz + xx) + h

    def fetch(n, src, dst):
        copy = pltpu.make_async_copy(src, dst, in_sem.at[n])
        copy.start()
        return copy

    first = [
        fetch(0, msa_gain_h, msa_gain),
        fetch(1, w_lhs_h, w_lhs),
        fetch(2, w_rhs_h, w_rhs),
    ]
    parts = [
        fetch(3 + n, msa_h.at[pl.ds(4 * n, 4)], msa.at[pl.ds(4 * n, 4)]) for n in range(4)
    ]
    mine = pl.ds(pl.multiple_of(h * 128, 128), 128)
    other = pl.ds(pl.multiple_of((1 - h) * 128, 128), 128)
    later = [
        fetch(7, w_final_h, w_final),
        fetch(8, pair_gain_h, gains.at[0]),
        fetch(9, tri_gain_h, gains.at[1]),
        fetch(10, coup_h.at[:, mine, :], coup16.at[pl.ds(h * 8, 8)]),
    ]
    for n, ref in enumerate((w_el_h, g_el_h, w_er_h, g_er_h, g_up_h, w_up_h)):
        fetch(11, ref, w_six.at[n])
    later.append(pltpu.make_async_copy(w_six, w_six, in_sem.at[11]))

    pending = []
    barrier = pltpu.get_barrier_semaphore()

    greeted = [sib]
    for k in (1, 2, 3):
        greeted += [dev((z + k) % 4, x), dev(z, (x + k) % 4)]
    for to in greeted:
        pl.semaphore_signal(barrier, inc=1, device_id={"dap": to}, device_id_type=MESH)

    for copy in first:
        copy.wait()
    wl4 = jnp.concatenate([w_lhs[...].astype(F32)] * 4, axis=0).T.astype(BF16)
    wrt = w_rhs[...]
    gain = msa_gain[...]

    def project(s):
        v = msa[s].astype(F32)
        mean = jnp.mean(v, axis=-1, keepdims=True)
        centred = v - mean
        spread = jnp.mean(centred * centred, axis=-1, keepdims=True)
        normed = (centred * lax.rsqrt(spread + 1e-05) * gain).astype(BF16)
        lp = jnp.dot(normed, wl4, preferred_element_type=F32)
        s_left[pl.ds(s, 256, stride=16), :] = lp
        rp = lax.dot_general(wrt, normed, NT, preferred_element_type=F32)
        s_right[0, pl.ds(s, 32, stride=16), :] = rp[:, :128]
        s_right[1, pl.ds(s, 32, stride=16), :] = rp[:, 128:]

    for n in range(4):
        parts[n].wait()
        pl.loop(4 * n, 4 * n + 4, unroll=2)(project)

    r_send[...] = s_right[1 - h].reshape(32, 16, 128).astype(BF16)

    lane = lax.broadcasted_iota(jnp.int32, (4, 16, 128), 2)

    @pl.loop(0, 16, unroll=2)
    def _(k):
        v = s_left[pl.ds(pl.multiple_of(k * 256, 256), 256), :].reshape(4, 4, 16, 128)
        v = jnp.where(
            lane < 32,
            v[:, 0],
            jnp.where(lane < 64, v[:, 1], jnp.where(lane < 96, v[:, 2], v[:, 3])),
        ).astype(BF16)
        for g in range(4):
            l_send[k, :, g * 128 : (g + 1) * 128] = v[g]

    pl.semaphore_wait(barrier, 7)

    def sent(ref, sem):
        pending.append(remote(ref, ref, sem, sib_recv.at[0], sib).wait_send)

    for k in (1, 2, 3):
        z2 = (z + k) % 4
        remote(
            l_send.at[pl.ds(4 * z2, 4)], l_stage.at[z], l_ssem.at[0], l_rsem.at[0], dev(z2, x)
        ).start()
    sent(l_stage.at[pl.ds(0, 3)], l_ssem.at[0])
    my16 = pl.ds(pl.multiple_of((2 * pos + h) * 16, 16), 16)
    sib_r = remote(r_send, r_all.at[:, my16, :], sib_send.at[0], sib_recv.at[0], sib)
    sib_r.start()
    sib_c = remote(
        coup_h.at[:, other, :],
        coup16.at[pl.ds(h * 8, 8)],
        sib_send.at[1],
        sib_recv.at[1],
        sib,
    )
    sib_c.start()
    pending += [sib_r.wait_send, sib_c.wait_send]
    r_all[:, my16, :] = s_right[h].reshape(32, 16, 128).astype(BF16)

    sib16 = pl.ds(pl.multiple_of((2 * pos + 1 - h) * 16, 16), 16)
    remote(r_send, r_all.at[:, sib16, :], sib_send.at[0], sib_recv.at[0], sib).wait_recv()

    def block(c, zz, xx):
        rows = pl.ds(pl.multiple_of((4 * xx + zz) * 32, 32), 32)
        return r_all.at[pl.ds(c * ND, ND), rows, :]

    def blocks(c, xx, half=None):
        rows = pl.ds(pl.multiple_of(xx * 128, 128), 128)
        if half is None:
            return r_all.at[pl.ds(c * ND, ND), rows, :]
        return r_all.at[pl.ds(c * ND + half * (ND // 2), ND // 2), rows, :]

    def z_copy(c, k):
        b = block(c, z, x)
        return remote(b, b, z_ssem, z_rsem.at[c], dev((z + k) % 4, x))

    def x_copy(c, zz, n):
        b = block(c, zz, x)
        return remote(b, b, x_ssem, x_rsem.at[c, n], dev(z, (x + 1 + 2 * n) % 4))

    def f_copy(c, n):
        b = blocks(c, (x + 3 - 2 * n) % 4, n)
        return remote(b, b, f_ssem, f_rsem.at[c, n], dev(z, (x + 1 + 2 * n) % 4))

    def z_wait(c):
        three = r_all.at[pl.ds(c * ND, ND), pl.ds(0, 96), :]
        remote(three, three, z_ssem, z_rsem.at[c], sib).wait_recv()

    def x_wait(c, n):
        b = blocks(c, (x + 3 - 2 * n) % 4)
        remote(b, b, x_ssem, x_rsem.at[c, n], sib).wait_recv()

    def f_wait(c, n):
        b = blocks(c, (x + 2) % 4, n)
        remote(b, b, f_ssem, f_rsem.at[c, n], sib).wait_recv()

    def z_start(c):
        for k in (1, 2, 3):
            z_copy(c, k).start()

    z_start(0)

    @pl.loop(0, CHUNKS)
    def _(c):
        for n in (0, 1):
            x_copy(c, z, n).start()

    z_start(1)
    l_stage[z] = l_send[pl.ds(4 * z, 4)]
    three = l_stage.at[pl.ds(0, 3)]
    remote(three, three, l_ssem.at[0], l_rsem.at[0], sib).wait_recv()
    for k in (1, 2, 3):
        x2 = (x + k) % 4
        remote(
            l_stage.at[:, x2],
            l_all.at[pl.ds(4 * x, 4), h],
            l_ssem.at[1],
            l_rsem.at[1],
            dev(z, x2),
        ).start()
    sent(three, l_ssem.at[1])
    l_all[pl.ds(4 * x, 4), h] = l_stage[:, x]
    sent(r_all.at[pl.ds(0, 3 * CHUNKS), pl.ds(0, 32 * ND), :], z_ssem)
    sent(r_all.at[pl.ds(0, 16)], x_ssem)
    sent(r_all.at[pl.ds(0, 8)], f_ssem)

    def spread(c):
        z_wait(c)
        for k in (1, 2, 3):
            for n in (0, 1):
                x_copy(c, (z + k) % 4, n).start()
        if c + 2 < CHUNKS:
            z_start(c + 2)

    def forward(c):
        for n in (0, 1):
            x_wait(c, n)
            f_copy(c, n).start()

    def finish(c):
        for n in (0, 1):
            f_wait(c, n)

        for p in range(ND // 2):
            d = c * ND + 2 * p
            rhs = jnp.concatenate([r_all[d], r_all[d + 1]], axis=1)
            o = jnp.dot(l_t[...], rhs, preferred_element_type=F32) * (1.0 / 512)
            o = o.astype(BF16)
            outer[:, 2 * p] = o[:, :128].reshape(16, 32, 128)
            outer[:, 2 * p + 1] = o[:, 128:].reshape(16, 32, 128)

        @pl.loop(0, 8, unroll=4)
        def _(a):
            rhs = jnp.concatenate(
                [outer[2 * a].reshape(128, 128), outer[2 * a + 1].reshape(128, 128)], axis=1
            )
            u = jnp.dot(w2[c], rhs, preferred_element_type=F32)
            mid[2 * a] += u[:, :128]
            mid[2 * a + 1] += u[:, 128:]

    spread(0)
    spread(1)

    for copy in later:
        copy.wait()
    s_tri[0:1024, :] = w_final[...].astype(F32)
    for d in range(32):
        part = s_tri[pl.ds(d, 32, stride=32), :]
        s_tri[1024 + d * 32 : 1024 + (d + 1) * 32, :] = part
    for b in range(8):
        w2[b] = s_tri[1024 + b * 128 : 1024 + (b + 1) * 128, :].T.astype(BF16)
    for b in range(4):
        t = w_six[b].astype(F32).T.astype(BF16)
        for g, n in enumerate(GROUPS):
            lo, n = 16 * sum(GROUPS[:g]), 16 * n
            w5[4 * lo + b * n : 4 * lo + (b + 1) * n, :] = t[lo : lo + n]
    for b in range(2):
        wu[b] = w_six[4 + b].astype(F32).T.astype(BF16)
    p_gain = column(gains[0])
    t_gain = column(gains[1])

    spread(2)
    forward(0)

    remote(
        coup_h.at[:, other, :],
        coup16.at[pl.ds((1 - h) * 8, 8)],
        sib_send.at[1],
        sib_recv.at[1],
        sib,
    ).wait_recv()
    eye = (
        lax.broadcasted_iota(jnp.int32, (128, 128), 0)
        == lax.broadcasted_iota(jnp.int32, (128, 128), 1)
    ).astype(F32).astype(BF16)

    @pl.loop(0, 16, unroll=4)
    def _(i):
        mid[i] = lax.dot_general(eye, coup16[i], NT, preferred_element_type=F32)

    forward(1)
    remote(three, three, l_ssem.at[1], l_rsem.at[1], sib).wait_recv()
    l_fwd = remote(l_all.at[:, h], l_all.at[:, h], sib_send.at[2], sib_recv.at[2], sib)
    l_fwd.start()
    pending.append(l_fwd.wait_send)
    spread(3)
    remote(
        l_all.at[:, 1 - h], l_all.at[:, 1 - h], sib_send.at[2], sib_recv.at[2], sib
    ).wait_recv()
    for b in range(4):
        l_t[b * 128 : (b + 1) * 128, :] = (
            l_all[:, :, :, b * 128 : (b + 1) * 128].reshape(512, 128).astype(F32).T.astype(BF16)
        )

    finish(0)
    forward(2)
    finish(1)
    for c in range(4, CHUNKS):
        spread(c)
        forward(c - 1)
        finish(c - 2)
    forward(CHUNKS - 1)
    finish(CHUNKS - 2)
    finish(CHUNKS - 1)


    zh = me // 16
    m_own = me % 16

    def e_near(g, m):
        return remote(
            e_send[g].at[m], e_recv[g].at[me], e_ssem, e_rsem.at[g], zh * 16 + m
        )

    def e_far(g, m):
        n = pl.ds(GROUPS[g], GROUPS[g])
        return remote(
            e_send[g].at[m, n],
            e_recv[g].at[me, n],
            e_ssem,
            e_rsem.at[g],
            (1 - zh) * 16 + m,
        )

    def edges(g, a):
        lo, n = 64 * sum(GROUPS[:g]), 16 * GROUPS[g]
        y = jnp.dot(w5[lo : lo + 4 * n], normed[a], preferred_element_type=F32)
        el = jax.nn.sigmoid(y[n : 2 * n]) * y[0:n]
        er = jax.nn.sigmoid(y[3 * n :]) * y[2 * n : 3 * n]
        for e in (0, 1):
            rows = pl.ds(2 * a + e, n, stride=16)
            s_el[rows, :] = el[:, e * 128 : (e + 1) * 128]
            s_er[rows, :] = er[:, e * 128 : (e + 1) * 128]

    def edges_send(g):
        n = GROUPS[g]

        @pl.loop(0, 16)
        def _(k):
            m = (m_own + k) % 16
            rows = pl.ds(pl.multiple_of(m * 16 * n, 16 * n), 16 * n)
            e_send[g][m, 0:n] = s_el[rows, :].reshape(n, 16, 128).astype(BF16)
            e_send[g][m, n : 2 * n] = s_er[rows, :].reshape(n, 16, 128).astype(BF16)
            e_far(g, m).start()

            @pl.when(k > 0)
            def _():
                e_near(g, m).start()

        e_recv[g][me] = e_send[g][m_own]

    @pl.loop(0, 8, unroll=2)
    def _(a):
        normed[a, :, 0:128] = norm_rows(mid[2 * a], p_gain)
        normed[a, :, 128:256] = norm_rows(mid[2 * a + 1], p_gain)
        edges(0, a)

    edges_send(0)

    for g in (1, 2):
        pl.loop(0, 8, unroll=2)(functools.partial(edges, g))
        edges_send(g)
    sent(r_all.at[pl.ds(0, 23), pl.ds(0, 256), :], e_ssem)

    @pl.loop(0, 8)
    def _(a):
        y = jax.nn.sigmoid(jnp.dot(wu[0], normed[a], preferred_element_type=F32))
        gate[2 * a] = y[:, :128]
        gate[2 * a + 1] = y[:, 128:]

    def t_copy(g, m):
        return remote(
            t_send[g].at[m // 2, m % 2],
            t_recv[g].at[m_own],
            t_ssem,
            t_rsem.at[g],
            zh * 16 + m,
        )

    for g, n in enumerate(GROUPS):
        every = r_all.at[pl.ds(0, 23), pl.ds(0, 32 * n), :]
        remote(every, every, e_ssem, e_rsem.at[g], sib).wait_recv()

        got = e_recv[g].reshape(2, 8, 2, 2 * n, 16, 128)
        for c in range(n):
            t = None
            for hh in (0, 1):
                lhs = got[zh, :, hh, c].reshape(128, 128)
                rhs = got[:, :, hh, n + c].reshape(256, 128)
                term = lax.dot_general(lhs, rhs, NT, preferred_element_type=F32)
                t = term if t is None else t + term
            t = t.astype(BF16)
            for hh in (0, 1):
                t_send[g][:, hh, c] = t[:, hh * 128 : (hh + 1) * 128].reshape(8, 16, 128)

        @pl.loop(1, 16)
        def _(k):
            t_copy(g, (m_own + k) % 16).start()

        t_recv[g][m_own] = t_send[g][m_own // 2, h]

    sent(r_all.at[pl.ds(0, 15), pl.ds(0, 128), :], t_ssem)
    for g, n in enumerate(GROUPS):
        fifteen = t_recv[g].at[pl.ds(0, 15)]
        remote(fifteen, fifteen, t_ssem, t_rsem.at[g], sib).wait_recv()
        lo = 256 * sum(GROUPS[:g])
        s_tri[lo : lo + 256 * n, :] = t_recv[g][...].reshape(256 * n, 128).astype(F32)


    def result(a):
        rows = [
            norm_rows(s_tri[pl.ds(2 * a + e, 128, stride=16), :], t_gain) for e in (0, 1)
        ]
        y = jnp.dot(wu[1], jnp.concatenate(rows, axis=1), preferred_element_type=F32)
        for e in (0, 1):
            i = 2 * a + e
            r = mid[i] + gate[i] * y[:, e * 128 : (e + 1) * 128]
            o_buf[i] = r.T.astype(BF16)

    @pl.loop(0, 4, unroll=2)
    def _(a):
        result(4 * (1 - h) + a)

    o_copy = remote(
        o_buf.at[pl.ds((1 - h) * 8, 8)], o_got, sib_send.at[3], sib_recv.at[3], sib
    )
    o_copy.start()
    pending.append(o_copy.wait_send)

    @pl.loop(0, 4, unroll=2)
    def _(a):
        result(4 * h + a)

    out[:, mine, :] = o_buf[pl.ds(h * 8, 8)]
    o_copy.wait_recv()
    out[:, other, :] = o_got[...]

    for wait in pending:
        wait()


def local(
    relative_embedding,
    coupling_features,
    relative_variance_multiplier,
    bilinear_lhs_projector,
    bilinear_rhs_projector,
    product_final_matrix,
    coupling_standard_scale,
    incoming_edge_matrix,
    incoming_edge_sigmoid,
    second_edge_matrix,
    second_edge_sigmoid,
    update_sigmoid_matrix,
    update_final_matrix,
    cubic_standard_scale,
):
    vm = pltpu.VMEM
    dma = pltpu.SemaphoreType.DMA
    return pl.pallas_call(
        kernel,
        out_shape=jax.ShapeDtypeStruct((8, 256, 128), BF16),
        in_specs=[pl.BlockSpec(memory_space=pl.ANY)] * 14,
        out_specs=pl.BlockSpec(memory_space=pltpu.VMEM),
        scratch_shapes=[
            vm((16, 256, 256), BF16),
            vm((1, 256), F32),
            vm((32, 256), BF16),
            vm((32, 256), BF16),
            vm((1024, 128), BF16),
            vm((2, 1, 128), F32),
            vm((6, 128, 128), BF16),
            vm((4096, 128), F32),
            vm((2, 512, 128), F32),
            vm((16, 16, 512), BF16),
            vm((4, 4, 16, 512), BF16),
            vm((16, 2, 16, 512), BF16),
            vm((512, 512), BF16),
            vm((32, 16, 128), BF16),
            vm((32, 512, 128), BF16),
            vm((16, ND, 32, 128), BF16),
            vm((16, 128, 128), BF16),
            vm((CHUNKS, 128, 128), BF16),
            vm((512, 128), BF16),
            vm((2, 128, 128), BF16),
            vm((16, 128, 128), F32),
            vm((16, 128, 128), F32),
            vm((8, 128, 256), BF16),
            vm((1024, 128), F32),
            vm((1024, 128), F32),
            [vm((16, 2 * n, 16, 128), BF16) for n in GROUPS],
            [vm((32, 2 * n, 16, 128), BF16) for n in GROUPS],
            [vm((8, 2, n, 16, 128), BF16) for n in GROUPS],
            [vm((16, n, 16, 128), BF16) for n in GROUPS],
            vm((2048, 128), F32),
            vm((16, 128, 128), BF16),
            vm((8, 128, 128), BF16),
            dma((12,)),
            dma((4,)),
            dma((4,)),
            dma((2,)),
            dma((2,)),
            dma,
            dma,
            dma,
            dma((CHUNKS,)),
            dma((CHUNKS, 2)),
            dma((CHUNKS, 2)),
            dma,
            dma((3,)),
            dma,
            dma((3,)),
        ],
        compiler_params=pltpu.CompilerParams(
            collective_id=0, has_side_effects=True, vmem_limit_bytes=60 * 1024 * 1024
        ),
    )(
        relative_embedding,
        coupling_features,
        relative_variance_multiplier.reshape(1, -1),
        bilinear_lhs_projector.T,
        bilinear_rhs_projector.T,
        product_final_matrix,
        coupling_standard_scale.reshape(1, -1),
        incoming_edge_matrix,
        incoming_edge_sigmoid,
        second_edge_matrix,
        second_edge_sigmoid,
        update_sigmoid_matrix,
        update_final_matrix,
        cubic_standard_scale.reshape(1, -1),
    )


def solution(mesh):
    rows = P(("batch", "dap"), None, None)
    return jax.shard_map(
        local,
        mesh=mesh,
        in_specs=(rows, rows) + (P(),) * 12,
        out_specs=rows,
        check_vma=False,
    )
```

```python
import functools

import jax
import jax.numpy as jnp
from jax import lax
from jax.experimental import pallas as pl
from jax.experimental.pallas import tpu as pltpu
from jax.sharding import PartitionSpec as P

MESH = pl.DeviceIdType.MESH
F32 = jnp.float32
BF16 = jnp.bfloat16
CHUNKS = 8
ND = 32 // CHUNKS
LAST = CHUNKS - 1
GROUPS = (2, 4, 2)
NT = (((1,), (1,)), ((), ()))


def remote(src, dst, send_sem, recv_sem, target):
    return pltpu.make_async_remote_copy(
        src_ref=src,
        dst_ref=dst,
        send_sem=send_sem,
        recv_sem=recv_sem,
        device_id={"dap": target},
        device_id_type=MESH,
    )


def column(row):
    return jnp.broadcast_to(row, (128, 128)).T


def norm_rows(v, gain):
    mean = jnp.mean(v, axis=0, keepdims=True)
    centred = v - mean
    spread = jnp.mean(centred * centred, axis=0, keepdims=True)
    return (centred * lax.rsqrt(spread + 1e-05) * gain).astype(BF16)


def kernel(
    msa_h,
    coup_h,
    msa_gain_h,
    w_lhs_h,
    w_rhs_h,
    w_final_h,
    pair_gain_h,
    w_el_h,
    g_el_h,
    w_er_h,
    g_er_h,
    g_up_h,
    w_up_h,
    tri_gain_h,
    out,
    msa,
    msa_gain,
    w_lhs,
    w_rhs,
    w_final,
    gains,
    w_six,
    s_left,
    s_right,
    l_send,
    l_stage,
    l_all,
    l_t,
    r_send,
    r_all,
    outer,
    coup16,
    w2,
    w5,
    wu,
    mid,
    gate,
    normed,
    s_el,
    s_er,
    e_send,
    e_recv,
    t_send,
    t_recv,
    s_tri,
    o_buf,
    o_got,
    in_sem,
    sib_send,
    sib_recv,
    l_ssem,
    l_rsem,
    z_ssem,
    x_ssem,
    f_ssem,
    z_rsem,
    e2_rsem,
    x_rsem,
    f_rsem,
    e_ssem,
    e_rsem,
    t_ssem,
    t_rsem,
):
    me = lax.axis_index("dap")
    h = me % 2
    q = me // 2
    x = q % 4
    z = q // 4
    sib = 2 * q + (1 - h)
    pos = 4 * x + z

    def dev(zz, xx):
        return 2 * (4 * zz + xx) + h

    def fetch(n, src, dst):
        copy = pltpu.make_async_copy(src, dst, in_sem.at[n])
        copy.start()
        return copy

    first = [
        fetch(0, msa_gain_h, msa_gain),
        fetch(1, w_lhs_h, w_lhs),
        fetch(2, w_rhs_h, w_rhs),
    ]
    parts = [
        fetch(3 + n, msa_h.at[pl.ds(4 * n, 4)], msa.at[pl.ds(4 * n, 4)]) for n in range(4)
    ]
    mine = pl.ds(pl.multiple_of(h * 128, 128), 128)
    other = pl.ds(pl.multiple_of((1 - h) * 128, 128), 128)
    later = [
        fetch(7, w_final_h, w_final),
        fetch(8, pair_gain_h, gains.at[0]),
        fetch(9, tri_gain_h, gains.at[1]),
        fetch(10, coup_h.at[:, mine, :], coup16.at[pl.ds(h * 8, 8)]),
    ]
    for n, ref in enumerate((w_el_h, g_el_h, w_er_h, g_er_h, g_up_h, w_up_h)):
        fetch(11, ref, w_six.at[n])
    later.append(pltpu.make_async_copy(w_six, w_six, in_sem.at[11]))

    pending = []
    barrier = pltpu.get_barrier_semaphore()

    greeted = [sib]
    for k in (1, 2, 3):
        greeted += [dev((z + k) % 4, x), dev(z, (x + k) % 4)]
    for to in greeted:
        pl.semaphore_signal(barrier, inc=1, device_id={"dap": to}, device_id_type=MESH)

    for copy in first:
        copy.wait()
    wl4 = jnp.concatenate([w_lhs[...].astype(F32)] * 4, axis=0).T.astype(BF16)
    wrt = w_rhs[...]
    gain = msa_gain[...]

    def project(s):
        v = msa[s].astype(F32)
        mean = jnp.mean(v, axis=-1, keepdims=True)
        centred = v - mean
        spread = jnp.mean(centred * centred, axis=-1, keepdims=True)
        normed = (centred * lax.rsqrt(spread + 1e-05) * gain).astype(BF16)
        lp = jnp.dot(normed, wl4, preferred_element_type=F32)
        s_left[pl.ds(s, 256, stride=16), :] = lp
        rp = lax.dot_general(wrt, normed, NT, preferred_element_type=F32)
        s_right[0, pl.ds(s, 32, stride=16), :] = rp[:, :128]
        s_right[1, pl.ds(s, 32, stride=16), :] = rp[:, 128:]

    for n in range(4):
        parts[n].wait()
        pl.loop(4 * n, 4 * n + 4, unroll=2)(project)

    r_send[...] = s_right[1 - h].reshape(32, 16, 128).astype(BF16)

    lane = lax.broadcasted_iota(jnp.int32, (4, 16, 128), 2)

    @pl.loop(0, 16, unroll=2)
    def _(k):
        v = s_left[pl.ds(pl.multiple_of(k * 256, 256), 256), :].reshape(4, 4, 16, 128)
        v = jnp.where(
            lane < 32,
            v[:, 0],
            jnp.where(lane < 64, v[:, 1], jnp.where(lane < 96, v[:, 2], v[:, 3])),
        ).astype(BF16)
        for g in range(4):
            l_send[k, :, g * 128 : (g + 1) * 128] = v[g]

    pl.semaphore_wait(barrier, 7)

    def sent(ref, sem):
        pending.append(remote(ref, ref, sem, sib_recv.at[0], sib).wait_send)

    for k in (1, 2, 3):
        z2 = (z + k) % 4
        remote(
            l_send.at[pl.ds(4 * z2, 4)], l_stage.at[z], l_ssem.at[0], l_rsem.at[0], dev(z2, x)
        ).start()
    sent(l_stage.at[pl.ds(0, 3)], l_ssem.at[0])
    def part(c, hh):
        rows = pl.ds(pl.multiple_of(32 * z + 16 * hh, 16), 16)
        return r_all.at[pl.ds(c * ND, ND), x, rows, :]

    all_mine = r_all.at[:, x, pl.ds(pl.multiple_of(32 * z + 16 * h, 16), 16), :]
    all_other = r_all.at[:, x, pl.ds(pl.multiple_of(32 * z + 16 * (1 - h), 16), 16), :]
    sib_r = remote(r_send, all_mine, sib_send.at[0], sib_recv.at[0], sib)
    sib_r.start()
    sib_c = remote(
        coup_h.at[:, other, :],
        coup16.at[pl.ds(h * 8, 8)],
        sib_send.at[1],
        sib_recv.at[1],
        sib,
    )
    sib_c.start()
    pending += [sib_r.wait_send, sib_c.wait_send]
    all_mine[...] = s_right[h].reshape(32, 16, 128).astype(BF16)

    def block(c, zz, xx):
        rows = pl.ds(pl.multiple_of(32 * zz, 32), 32)
        return r_all.at[pl.ds(c * ND, ND), xx, rows, :]

    def blocks(c, xx, half=None):
        if half is None:
            return r_all.at[pl.ds(c * ND, ND), xx]
        return r_all.at[pl.ds(c * ND + half * (ND // 2), ND // 2), xx]

    def row(zz):
        rows = pl.ds(pl.multiple_of(32 * zz, 32), 32)
        return r_all.at[pl.ds(LAST * ND, ND), :, rows, :]

    def row_half(xx, half):
        rows = pl.ds(pl.multiple_of(32 * z, 32), 32)
        return r_all.at[pl.ds(LAST * ND + half * (ND // 2), ND // 2), xx, rows, :]

    def own_start(c, hh):
        for n in (0, 1):
            b = part(c, hh)
            remote(b, b, x_ssem, x_rsem.at[c, n], dev(z, (x + 1 + 2 * n) % 4)).start()

    def z_copy(c, k):
        b = block(c, z, x)
        return remote(b, b, z_ssem, z_rsem.at[c], dev((z + k) % 4, x))

    def x_copy(c, zz, n):
        b = block(c, zz, x)
        return remote(b, b, x_ssem, x_rsem.at[c, n], dev(z, (x + 1 + 2 * n) % 4))

    def f_copy(c, n):
        b = blocks(c, (x + 3 - 2 * n) % 4, n)
        return remote(b, b, f_ssem, f_rsem.at[c, n], dev(z, (x + 1 + 2 * n) % 4))

    at_end = z % 3 == 0
    inner = z % 3 != 0
    end = 3 * (z // 2)

    def z_relay(c):
        b = block(c, 3 - end, x)
        return remote(b, b, z_ssem, e2_rsem.at[c], dev(end, x))

    def z_wait(c, n):
        b = r_all.at[pl.ds(c * ND, ND), 0, pl.ds(0, 32 * n), :]
        remote(b, b, z_ssem, z_rsem.at[c], sib).wait_recv()

    def x_wait(c, n):
        b = blocks(c, (x + 3 - 2 * n) % 4)
        remote(b, b, x_ssem, x_rsem.at[c, n], sib).wait_recv()

    def f_wait(c, n):
        b = blocks(c, (x + 2) % 4, n)
        remote(b, b, f_ssem, f_rsem.at[c, n], sib).wait_recv()

    def z_start(c):
        for k in (1, 2, 3):

            @pl.when(((z + k) % 4 - z) * ((z + k) % 4 - z) < 9)
            def _():
                z_copy(c, k).start()

    def row_start():
        for k in (1, 2, 3):
            to = (z + k) % 4

            @pl.when((to - z) * (to - z) < 9)
            def _():
                remote(row(z), row(z), z_ssem, z_rsem.at[LAST], dev(to, x)).start()

    def row_forward():
        for n in (0, 1):
            b = block(LAST, z, (x + 3 - 2 * n) % 4)
            remote(b, b, x_ssem, x_rsem.at[LAST, n], sib).wait_recv()
            b = row_half((x + 3 - 2 * n) % 4, n)
            remote(b, b, f_ssem, f_rsem.at[LAST, n], dev(z, (x + 1 + 2 * n) % 4)).start()

    def row_forwarded():
        for n in (0, 1):
            b = row_half((x + 2) % 4, n)
            remote(b, b, f_ssem, f_rsem.at[LAST, n], sib).wait_recv()

    def row_relay():
        @pl.when(inner)
        def _():
            ref = r_all.at[pl.ds(0, 3 * ND), 0]
            remote(ref, ref, z_ssem, z_rsem.at[LAST], sib).wait_recv()
            b = row(3 - end)
            remote(b, b, z_ssem, e2_rsem.at[LAST], dev(end, x)).start()

        @pl.when(at_end)
        def _():
            ref = r_all.at[pl.ds(0, 2 * ND), 0]
            remote(ref, ref, z_ssem, z_rsem.at[LAST], sib).wait_recv()

    def row_relayed():
        @pl.when(at_end)
        def _():
            b = row(3 - z)
            remote(b, b, z_ssem, e2_rsem.at[LAST], sib).wait_recv()

    @pl.loop(0, CHUNKS)
    def _(k):
        own_start((k + LAST) % CHUNKS, h)

    remote(r_send, all_other, sib_send.at[0], sib_recv.at[0], sib).wait_recv()
    z_start(0)

    @pl.loop(0, CHUNKS)
    def _(k):
        own_start((k + LAST) % CHUNKS, 1 - h)

    z_start(1)
    l_stage[z] = l_send[pl.ds(4 * z, 4)]
    three = l_stage.at[pl.ds(0, 3)]
    remote(three, three, l_ssem.at[0], l_rsem.at[0], sib).wait_recv()
    for k in (1, 2, 3):
        x2 = (x + k) % 4
        remote(
            l_stage.at[:, x2],
            l_all.at[pl.ds(4 * x, 4), h],
            l_ssem.at[1],
            l_rsem.at[1],
            dev(z, x2),
        ).start()
    sent(three, l_ssem.at[1])
    l_all[pl.ds(4 * x, 4), h] = l_stage[:, x]

    def z_sent():
        for here, n in ((at_end, 2), (inner, 4)):

            @pl.when(here)
            def _():
                ref = r_all.at[pl.ds(0, CHUNKS + 3), pl.ds(0, n)]
                remote(ref, ref, z_ssem, sib_recv.at[0], sib).wait_send()

    pending.append(z_sent)
    sent(r_all.at[pl.ds(0, 4 * LAST + 1), pl.ds(0, 2)], x_ssem)
    sent(r_all.at[pl.ds(0, 4 * LAST + 1), 0], f_ssem)

    def spread(c):
        @pl.when(inner)
        def _():
            z_wait(c, 3)
            z_relay(c).start()

        @pl.when(at_end)
        def _():
            z_wait(c, 2)

        if c + 2 < LAST:
            z_start(c + 2)
        for k in (1, 2, 3):
            zz = (z + k) % 4

            @pl.when((zz - z) * (zz - z) < 9)
            def _():
                for n in (0, 1):
                    x_copy(c, zz, n).start()

    def spread_end(c):
        @pl.when(at_end)
        def _():
            b = block(c, 3 - z, x)
            remote(b, b, z_ssem, e2_rsem.at[c], sib).wait_recv()
            for n in (0, 1):
                x_copy(c, 3 - z, n).start()

    def forward(c):
        for n in (0, 1):
            x_wait(c, n)
            f_copy(c, n).start()

    def finish(c):
        if c == LAST:
            row_relayed()
        else:
            for n in (0, 1):
                f_wait(c, n)

        for p in range(ND // 2):
            d = c * ND + 2 * p
            rhs = jnp.concatenate(
                [r_all[d].reshape(512, 128), r_all[d + 1].reshape(512, 128)], axis=1
            )
            o = jnp.dot(l_t[...], rhs, preferred_element_type=F32) * (1.0 / 512)
            o = o.astype(BF16)
            outer[:, 2 * p] = o[:, :128].reshape(16, 32, 128)
            outer[:, 2 * p + 1] = o[:, 128:].reshape(16, 32, 128)

        @pl.loop(0, 8, unroll=4)
        def _(a):
            rhs = jnp.concatenate(
                [outer[2 * a].reshape(128, 128), outer[2 * a + 1].reshape(128, 128)], axis=1
            )
            u = jnp.dot(w2[c], rhs, preferred_element_type=F32)
            mid[2 * a] += u[:, :128]
            mid[2 * a + 1] += u[:, 128:]

    spread(0)
    spread_end(0)
    spread(1)
    spread_end(1)
    row_forward()

    for copy in later:
        copy.wait()
    s_tri[0:1024, :] = w_final[...].astype(F32)
    for d in range(32):
        part = s_tri[pl.ds(d, 32, stride=32), :]
        s_tri[1024 + d * 32 : 1024 + (d + 1) * 32, :] = part
    for b in range(8):
        w2[b] = s_tri[1024 + b * 128 : 1024 + (b + 1) * 128, :].T.astype(BF16)
    for b in range(4):
        t = w_six[b].astype(F32).T.astype(BF16)
        for g, n in enumerate(GROUPS):
            lo, n = 16 * sum(GROUPS[:g]), 16 * n
            w5[4 * lo + b * n : 4 * lo + (b + 1) * n, :] = t[lo : lo + n]
    for b in range(2):
        wu[b] = w_six[4 + b].astype(F32).T.astype(BF16)
    p_gain = column(gains[0])
    t_gain = column(gains[1])

    spread(2)
    forward(0)
    spread_end(2)

    remote(
        coup_h.at[:, other, :],
        coup16.at[pl.ds((1 - h) * 8, 8)],
        sib_send.at[1],
        sib_recv.at[1],
        sib,
    ).wait_recv()
    eye = (
        lax.broadcasted_iota(jnp.int32, (128, 128), 0)
        == lax.broadcasted_iota(jnp.int32, (128, 128), 1)
    ).astype(F32).astype(BF16)

    @pl.loop(0, 16, unroll=4)
    def _(i):
        mid[i] = lax.dot_general(eye, coup16[i], NT, preferred_element_type=F32)

    forward(1)
    remote(three, three, l_ssem.at[1], l_rsem.at[1], sib).wait_recv()
    l_fwd = remote(l_all.at[:, h], l_all.at[:, h], sib_send.at[2], sib_recv.at[2], sib)
    l_fwd.start()
    pending.append(l_fwd.wait_send)
    spread(3)
    spread_end(3)
    remote(
        l_all.at[:, 1 - h], l_all.at[:, 1 - h], sib_send.at[2], sib_recv.at[2], sib
    ).wait_recv()
    for b in range(4):
        l_t[b * 128 : (b + 1) * 128, :] = (
            l_all[:, :, :, b * 128 : (b + 1) * 128].reshape(512, 128).astype(F32).T.astype(BF16)
        )

    finish(0)
    row_forwarded()
    for c in range(4, LAST):
        spread(c)
        if c == 4:
            row_start()
        spread_end(c)
        forward(c - 2)
        finish(c - 3)
    row_relay()
    forward(LAST - 2)
    finish(LAST - 3)
    forward(LAST - 1)
    finish(LAST)
    finish(LAST - 2)
    finish(LAST - 1)


    zh = me // 16
    m_own = me % 16

    def e_near(g, m):
        return remote(
            e_send[g].at[m], e_recv[g].at[me], e_ssem, e_rsem.at[g], zh * 16 + m
        )

    def e_far(g, m):
        n = pl.ds(GROUPS[g], GROUPS[g])
        return remote(
            e_send[g].at[m, n],
            e_recv[g].at[me, n],
            e_ssem,
            e_rsem.at[g],
            (1 - zh) * 16 + m,
        )

    def edges(g, a):
        lo, n = 64 * sum(GROUPS[:g]), 16 * GROUPS[g]
        y = jnp.dot(w5[lo : lo + 4 * n], normed[a], preferred_element_type=F32)
        el = jax.nn.sigmoid(y[n : 2 * n]) * y[0:n]
        er = jax.nn.sigmoid(y[3 * n :]) * y[2 * n : 3 * n]
        for e in (0, 1):
            rows = pl.ds(2 * a + e, n, stride=16)
            s_el[rows, :] = el[:, e * 128 : (e + 1) * 128]
            s_er[rows, :] = er[:, e * 128 : (e + 1) * 128]

    def edges_send(g):
        n = GROUPS[g]

        @pl.loop(0, 16)
        def _(k):
            m = (m_own + k) % 16
            rows = pl.ds(pl.multiple_of(m * 16 * n, 16 * n), 16 * n)
            e_send[g][m, 0:n] = s_el[rows, :].reshape(n, 16, 128).astype(BF16)
            e_send[g][m, n : 2 * n] = s_er[rows, :].reshape(n, 16, 128).astype(BF16)
            e_far(g, m).start()

            @pl.when(k > 0)
            def _():
                e_near(g, m).start()

        e_recv[g][me] = e_send[g][m_own]

    @pl.loop(0, 8, unroll=2)
    def _(a):
        normed[a, :, 0:128] = norm_rows(mid[2 * a], p_gain)
        normed[a, :, 128:256] = norm_rows(mid[2 * a + 1], p_gain)
        edges(0, a)

    edges_send(0)

    for g in (1, 2):
        pl.loop(0, 8, unroll=2)(functools.partial(edges, g))
        edges_send(g)
    sent(r_all.at[pl.ds(0, 23), pl.ds(0, 2)], e_ssem)

    @pl.loop(0, 8)
    def _(a):
        y = jax.nn.sigmoid(jnp.dot(wu[0], normed[a], preferred_element_type=F32))
        gate[2 * a] = y[:, :128]
        gate[2 * a + 1] = y[:, 128:]

    def t_copy(g, m):
        return remote(
            t_send[g].at[m // 2, m % 2],
            t_recv[g].at[m_own],
            t_ssem,
            t_rsem.at[g],
            zh * 16 + m,
        )

    for g, n in enumerate(GROUPS):
        every = r_all.at[pl.ds(0, 23), 0, pl.ds(0, 32 * n), :]
        remote(every, every, e_ssem, e_rsem.at[g], sib).wait_recv()

        got = e_recv[g].reshape(2, 8, 2, 2 * n, 16, 128)
        for c in range(n):
            t = None
            for hh in (0, 1):
                lhs = got[zh, :, hh, c].reshape(128, 128)
                rhs = got[:, :, hh, n + c].reshape(256, 128)
                term = lax.dot_general(lhs, rhs, NT, preferred_element_type=F32)
                t = term if t is None else t + term
            t = t.astype(BF16)
            for hh in (0, 1):
                t_send[g][:, hh, c] = t[:, hh * 128 : (hh + 1) * 128].reshape(8, 16, 128)

        @pl.loop(1, 16)
        def _(k):
            t_copy(g, (m_own + k) % 16).start()

        t_recv[g][m_own] = t_send[g][m_own // 2, h]

    sent(r_all.at[pl.ds(0, 15), 0], t_ssem)
    for g, n in enumerate(GROUPS):
        fifteen = t_recv[g].at[pl.ds(0, 15)]
        remote(fifteen, fifteen, t_ssem, t_rsem.at[g], sib).wait_recv()
        lo = 256 * sum(GROUPS[:g])
        s_tri[lo : lo + 256 * n, :] = t_recv[g][...].reshape(256 * n, 128).astype(F32)


    def result(a):
        rows = [
            norm_rows(s_tri[pl.ds(2 * a + e, 128, stride=16), :], t_gain) for e in (0, 1)
        ]
        y = jnp.dot(wu[1], jnp.concatenate(rows, axis=1), preferred_element_type=F32)
        for e in (0, 1):
            i = 2 * a + e
            r = mid[i] + gate[i] * y[:, e * 128 : (e + 1) * 128]
            o_buf[i] = r.T.astype(BF16)

    @pl.loop(0, 4, unroll=2)
    def _(a):
        result(4 * (1 - h) + a)

    o_copy = remote(
        o_buf.at[pl.ds((1 - h) * 8, 8)], o_got, sib_send.at[3], sib_recv.at[3], sib
    )
    o_copy.start()
    pending.append(o_copy.wait_send)

    @pl.loop(0, 4, unroll=2)
    def _(a):
        result(4 * h + a)

    out[:, mine, :] = o_buf[pl.ds(h * 8, 8)]
    o_copy.wait_recv()
    out[:, other, :] = o_got[...]

    for wait in pending:
        wait()


def local(
    relative_embedding,
    coupling_features,
    relative_variance_multiplier,
    bilinear_lhs_projector,
    bilinear_rhs_projector,
    product_final_matrix,
    coupling_standard_scale,
    incoming_edge_matrix,
    incoming_edge_sigmoid,
    second_edge_matrix,
    second_edge_sigmoid,
    update_sigmoid_matrix,
    update_final_matrix,
    cubic_standard_scale,
):
    vm = pltpu.VMEM
    dma = pltpu.SemaphoreType.DMA
    return pl.pallas_call(
        kernel,
        out_shape=jax.ShapeDtypeStruct((8, 256, 128), BF16),
        in_specs=[pl.BlockSpec(memory_space=pl.ANY)] * 14,
        out_specs=pl.BlockSpec(memory_space=pltpu.VMEM),
        scratch_shapes=[
            vm((16, 256, 256), BF16),
            vm((1, 256), F32),
            vm((32, 256), BF16),
            vm((32, 256), BF16),
            vm((1024, 128), BF16),
            vm((2, 1, 128), F32),
            vm((6, 128, 128), BF16),
            vm((4096, 128), F32),
            vm((2, 512, 128), F32),
            vm((16, 16, 512), BF16),
            vm((4, 4, 16, 512), BF16),
            vm((16, 2, 16, 512), BF16),
            vm((512, 512), BF16),
            vm((32, 16, 128), BF16),
            vm((32, 4, 128, 128), BF16),
            vm((16, ND, 32, 128), BF16),
            vm((16, 128, 128), BF16),
            vm((CHUNKS, 128, 128), BF16),
            vm((512, 128), BF16),
            vm((2, 128, 128), BF16),
            vm((16, 128, 128), F32),
            vm((16, 128, 128), F32),
            vm((8, 128, 256), BF16),
            vm((1024, 128), F32),
            vm((1024, 128), F32),
            [vm((16, 2 * n, 16, 128), BF16) for n in GROUPS],
            [vm((32, 2 * n, 16, 128), BF16) for n in GROUPS],
            [vm((8, 2, n, 16, 128), BF16) for n in GROUPS],
            [vm((16, n, 16, 128), BF16) for n in GROUPS],
            vm((2048, 128), F32),
            vm((16, 128, 128), BF16),
            vm((8, 128, 128), BF16),
            dma((12,)),
            dma((4,)),
            dma((4,)),
            dma((2,)),
            dma((2,)),
            dma,
            dma,
            dma,
            dma((CHUNKS,)),
            dma((CHUNKS,)),
            dma((CHUNKS, 2)),
            dma((CHUNKS, 2)),
            dma,
            dma((3,)),
            dma,
            dma((3,)),
        ],
        compiler_params=pltpu.CompilerParams(
            collective_id=0, has_side_effects=True, vmem_limit_bytes=60 * 1024 * 1024
        ),
    )(
        relative_embedding,
        coupling_features,
        relative_variance_multiplier.reshape(1, -1),
        bilinear_lhs_projector.T,
        bilinear_rhs_projector.T,
        product_final_matrix,
        coupling_standard_scale.reshape(1, -1),
        incoming_edge_matrix,
        incoming_edge_sigmoid,
        second_edge_matrix,
        second_edge_sigmoid,
        update_sigmoid_matrix,
        update_final_matrix,
        cubic_standard_scale.reshape(1, -1),
    )


def solution(mesh):
    rows = P(("batch", "dap"), None, None)
    return jax.shard_map(
        local,
        mesh=mesh,
        in_specs=(rows, rows) + (P(),) * 12,
        out_specs=rows,
        check_vma=False,
    )
```

```python
import functools

import jax
import jax.numpy as jnp
from jax import lax
from jax.experimental import pallas as pl
from jax.experimental.pallas import tpu as pltpu
from jax.sharding import PartitionSpec as P

MESH = pl.DeviceIdType.MESH
F32 = jnp.float32
BF16 = jnp.bfloat16
CHUNKS = 8
ND = 32 // CHUNKS
LAST = CHUNKS - 1
GROUPS = (2, 3, 2, 1)
NT = (((1,), (1,)), ((), ()))


def remote(src, dst, send_sem, recv_sem, target):
    return pltpu.make_async_remote_copy(
        src_ref=src,
        dst_ref=dst,
        send_sem=send_sem,
        recv_sem=recv_sem,
        device_id={"dap": target},
        device_id_type=MESH,
    )


def column(row):
    return jnp.broadcast_to(row, (128, 128)).T


def norm_rows(v, gain):
    mean = jnp.mean(v, axis=0, keepdims=True)
    centred = v - mean
    spread = jnp.mean(centred * centred, axis=0, keepdims=True)
    return (centred * lax.rsqrt(spread + 1e-05) * gain).astype(BF16)


def kernel(
    msa_h,
    coup_h,
    msa_gain_h,
    w_lhs_h,
    w_rhs_h,
    w_final_h,
    pair_gain_h,
    w_el_h,
    g_el_h,
    w_er_h,
    g_er_h,
    g_up_h,
    w_up_h,
    tri_gain_h,
    out,
    msa,
    msa_gain,
    w_lhs,
    w_rhs,
    w_final,
    gains,
    w_six,
    s_left,
    s_right,
    l_send,
    l_stage,
    l_all,
    l_t,
    r_send,
    r_all,
    outer,
    coup16,
    w2,
    w5,
    wu,
    mid,
    gate,
    normed,
    s_el,
    s_er,
    e_send,
    e_recv,
    t_send,
    t_recv,
    s_tri,
    o_buf,
    o_got,
    in_sem,
    sib_send,
    sib_recv,
    l_ssem,
    l_rsem,
    z_ssem,
    x_ssem,
    f_ssem,
    z_rsem,
    e2_rsem,
    x_rsem,
    f_rsem,
    e_ssem,
    e_rsem,
    t_ssem,
    t_rsem,
):
    me = lax.axis_index("dap")
    h = me % 2
    q = me // 2
    x = q % 4
    z = q // 4
    sib = 2 * q + (1 - h)
    pos = 4 * x + z

    def dev(zz, xx):
        return 2 * (4 * zz + xx) + h

    def fetch(n, src, dst):
        copy = pltpu.make_async_copy(src, dst, in_sem.at[n])
        copy.start()
        return copy

    first = [
        fetch(0, msa_gain_h, msa_gain),
        fetch(1, w_lhs_h, w_lhs),
        fetch(2, w_rhs_h, w_rhs),
    ]
    parts = [
        fetch(3 + n, msa_h.at[pl.ds(4 * n, 4)], msa.at[pl.ds(4 * n, 4)]) for n in range(4)
    ]
    mine = pl.ds(pl.multiple_of(h * 128, 128), 128)
    other = pl.ds(pl.multiple_of((1 - h) * 128, 128), 128)
    later = [
        fetch(7, w_final_h, w_final),
        fetch(8, pair_gain_h, gains.at[0]),
        fetch(9, tri_gain_h, gains.at[1]),
        fetch(10, coup_h.at[:, mine, :], coup16.at[pl.ds(h * 8, 8)]),
    ]
    for n, ref in enumerate((w_el_h, g_el_h, w_er_h, g_er_h, g_up_h, w_up_h)):
        fetch(11, ref, w_six.at[n])
    later.append(pltpu.make_async_copy(w_six, w_six, in_sem.at[11]))

    pending = []
    barrier = pltpu.get_barrier_semaphore()

    greeted = [sib]
    for k in (1, 2, 3):
        greeted += [dev((z + k) % 4, x), dev(z, (x + k) % 4)]
    for to in greeted:
        pl.semaphore_signal(barrier, inc=1, device_id={"dap": to}, device_id_type=MESH)

    for copy in first:
        copy.wait()
    wl4 = jnp.concatenate([w_lhs[...].astype(F32)] * 4, axis=0).T.astype(BF16)
    wrt = w_rhs[...]
    gain = msa_gain[...]

    def project(s):
        v = msa[s].astype(F32)
        mean = jnp.mean(v, axis=-1, keepdims=True)
        centred = v - mean
        spread = jnp.mean(centred * centred, axis=-1, keepdims=True)
        normed = (centred * lax.rsqrt(spread + 1e-05) * gain).astype(BF16)
        lp = jnp.dot(normed, wl4, preferred_element_type=F32)
        s_left[pl.ds(s, 256, stride=16), :] = lp
        rp = lax.dot_general(wrt, normed, NT, preferred_element_type=F32)
        s_right[0, pl.ds(s, 32, stride=16), :] = rp[:, :128]
        s_right[1, pl.ds(s, 32, stride=16), :] = rp[:, 128:]

    for n in range(4):
        parts[n].wait()
        pl.loop(4 * n, 4 * n + 4, unroll=2)(project)

    r_send[...] = s_right[1 - h].reshape(32, 16, 128).astype(BF16)

    lane = lax.broadcasted_iota(jnp.int32, (4, 16, 128), 2)

    @pl.loop(0, 16, unroll=2)
    def _(k):
        v = s_left[pl.ds(pl.multiple_of(k * 256, 256), 256), :].reshape(4, 4, 16, 128)
        v = jnp.where(
            lane < 32,
            v[:, 0],
            jnp.where(lane < 64, v[:, 1], jnp.where(lane < 96, v[:, 2], v[:, 3])),
        ).astype(BF16)
        for g in range(4):
            l_send[k, :, g * 128 : (g + 1) * 128] = v[g]

    pl.semaphore_wait(barrier, 7)

    def sent(ref, sem):
        pending.append(remote(ref, ref, sem, sib_recv.at[0], sib).wait_send)

    for k in (1, 2, 3):
        z2 = (z + k) % 4
        remote(
            l_send.at[pl.ds(4 * z2, 4)], l_stage.at[z], l_ssem.at[0], l_rsem.at[0], dev(z2, x)
        ).start()
    sent(l_stage.at[pl.ds(0, 3)], l_ssem.at[0])
    def part(c, hh):
        rows = pl.ds(pl.multiple_of(32 * z + 16 * hh, 16), 16)
        return r_all.at[pl.ds(c * ND, ND), x, rows, :]

    all_mine = r_all.at[:, x, pl.ds(pl.multiple_of(32 * z + 16 * h, 16), 16), :]
    all_other = r_all.at[:, x, pl.ds(pl.multiple_of(32 * z + 16 * (1 - h), 16), 16), :]
    sib_r = remote(r_send, all_mine, sib_send.at[0], sib_recv.at[0], sib)
    sib_r.start()
    sib_c = remote(
        coup_h.at[:, other, :],
        coup16.at[pl.ds(h * 8, 8)],
        sib_send.at[1],
        sib_recv.at[1],
        sib,
    )
    sib_c.start()
    pending += [sib_r.wait_send, sib_c.wait_send]
    all_mine[...] = s_right[h].reshape(32, 16, 128).astype(BF16)

    def block(c, zz, xx):
        rows = pl.ds(pl.multiple_of(32 * zz, 32), 32)
        return r_all.at[pl.ds(c * ND, ND), xx, rows, :]

    def blocks(c, xx, half=None):
        if half is None:
            return r_all.at[pl.ds(c * ND, ND), xx]
        return r_all.at[pl.ds(c * ND + half * (ND // 2), ND // 2), xx]

    def row(zz):
        rows = pl.ds(pl.multiple_of(32 * zz, 32), 32)
        return r_all.at[pl.ds(LAST * ND, ND), :, rows, :]

    def row_half(xx, half):
        rows = pl.ds(pl.multiple_of(32 * z, 32), 32)
        return r_all.at[pl.ds(LAST * ND + half * (ND // 2), ND // 2), xx, rows, :]

    def own_start(c, hh):
        for n in (0, 1):
            b = part(c, hh)
            remote(b, b, x_ssem, x_rsem.at[c, n], dev(z, (x + 1 + 2 * n) % 4)).start()

    def z_copy(c, k):
        b = block(c, z, x)
        return remote(b, b, z_ssem, z_rsem.at[c], dev((z + k) % 4, x))

    def x_copy(c, zz, n):
        b = block(c, zz, x)
        return remote(b, b, x_ssem, x_rsem.at[c, n], dev(z, (x + 1 + 2 * n) % 4))

    def f_copy(c, n):
        b = blocks(c, (x + 3 - 2 * n) % 4, n)
        return remote(b, b, f_ssem, f_rsem.at[c, n], dev(z, (x + 1 + 2 * n) % 4))

    at_end = z % 3 == 0
    inner = z % 3 != 0
    end = 3 * (z // 2)

    def z_relay(c):
        b = block(c, 3 - end, x)
        return remote(b, b, z_ssem, e2_rsem.at[c], dev(end, x))

    def z_wait(c, n):
        b = r_all.at[pl.ds(c * ND, ND), 0, pl.ds(0, 32 * n), :]
        remote(b, b, z_ssem, z_rsem.at[c], sib).wait_recv()

    def x_wait(c, n):
        b = blocks(c, (x + 3 - 2 * n) % 4)
        remote(b, b, x_ssem, x_rsem.at[c, n], sib).wait_recv()

    def f_wait(c, n):
        b = blocks(c, (x + 2) % 4, n)
        remote(b, b, f_ssem, f_rsem.at[c, n], sib).wait_recv()

    def z_start(c):
        for k in (1, 2, 3):

            @pl.when(((z + k) % 4 - z) * ((z + k) % 4 - z) < 9)
            def _():
                z_copy(c, k).start()

    def row_start():
        for k in (1, 2, 3):
            to = (z + k) % 4

            @pl.when((to - z) * (to - z) < 9)
            def _():
                remote(row(z), row(z), z_ssem, z_rsem.at[LAST], dev(to, x)).start()

    def row_forward():
        for n in (0, 1):
            b = block(LAST, z, (x + 3 - 2 * n) % 4)
            remote(b, b, x_ssem, x_rsem.at[LAST, n], sib).wait_recv()
            b = row_half((x + 3 - 2 * n) % 4, n)
            remote(b, b, f_ssem, f_rsem.at[LAST, n], dev(z, (x + 1 + 2 * n) % 4)).start()

    def row_forwarded():
        for n in (0, 1):
            b = row_half((x + 2) % 4, n)
            remote(b, b, f_ssem, f_rsem.at[LAST, n], sib).wait_recv()

    def row_relay():
        @pl.when(inner)
        def _():
            ref = r_all.at[pl.ds(0, 3 * ND), 0]
            remote(ref, ref, z_ssem, z_rsem.at[LAST], sib).wait_recv()
            b = row(3 - end)
            remote(b, b, z_ssem, e2_rsem.at[LAST], dev(end, x)).start()

        @pl.when(at_end)
        def _():
            ref = r_all.at[pl.ds(0, 2 * ND), 0]
            remote(ref, ref, z_ssem, z_rsem.at[LAST], sib).wait_recv()

    def row_relayed():
        @pl.when(at_end)
        def _():
            b = row(3 - z)
            remote(b, b, z_ssem, e2_rsem.at[LAST], sib).wait_recv()

    @pl.loop(0, CHUNKS)
    def _(k):
        own_start((k + LAST) % CHUNKS, h)

    remote(r_send, all_other, sib_send.at[0], sib_recv.at[0], sib).wait_recv()
    z_start(0)

    @pl.loop(0, CHUNKS)
    def _(k):
        own_start((k + LAST) % CHUNKS, 1 - h)

    z_start(1)
    l_stage[z] = l_send[pl.ds(4 * z, 4)]
    three = l_stage.at[pl.ds(0, 3)]
    remote(three, three, l_ssem.at[0], l_rsem.at[0], sib).wait_recv()
    for k in (1, 2, 3):
        x2 = (x + k) % 4
        remote(
            l_stage.at[:, x2],
            l_all.at[pl.ds(4 * x, 4), h],
            l_ssem.at[1],
            l_rsem.at[1],
            dev(z, x2),
        ).start()
    sent(three, l_ssem.at[1])
    l_all[pl.ds(4 * x, 4), h] = l_stage[:, x]

    def z_sent():
        for here, n in ((at_end, 2), (inner, 4)):

            @pl.when(here)
            def _():
                ref = r_all.at[pl.ds(0, CHUNKS + 3), pl.ds(0, n)]
                remote(ref, ref, z_ssem, sib_recv.at[0], sib).wait_send()

    pending.append(z_sent)
    sent(r_all.at[pl.ds(0, 4 * LAST + 1), pl.ds(0, 2)], x_ssem)
    sent(r_all.at[pl.ds(0, 4 * LAST + 1), 0], f_ssem)

    def spread(c):
        @pl.when(inner)
        def _():
            z_wait(c, 3)
            z_relay(c).start()

        @pl.when(at_end)
        def _():
            z_wait(c, 2)

        if c + 2 < LAST:
            z_start(c + 2)
        for k in (1, 2, 3):
            zz = (z + k) % 4

            @pl.when((zz - z) * (zz - z) < 9)
            def _():
                for n in (0, 1):
                    x_copy(c, zz, n).start()

    def spread_end(c):
        @pl.when(at_end)
        def _():
            b = block(c, 3 - z, x)
            remote(b, b, z_ssem, e2_rsem.at[c], sib).wait_recv()
            for n in (0, 1):
                x_copy(c, 3 - z, n).start()

    def forward(c):
        for n in (0, 1):
            x_wait(c, n)
            f_copy(c, n).start()

    def finish(c):
        if c == LAST:
            row_relayed()
        else:
            for n in (0, 1):
                f_wait(c, n)

        for p in range(ND // 2):
            d = c * ND + 2 * p
            rhs = jnp.concatenate(
                [r_all[d].reshape(512, 128), r_all[d + 1].reshape(512, 128)], axis=1
            )
            o = jnp.dot(l_t[...], rhs, preferred_element_type=F32) * (1.0 / 512)
            o = o.astype(BF16)
            outer[:, 2 * p] = o[:, :128].reshape(16, 32, 128)
            outer[:, 2 * p + 1] = o[:, 128:].reshape(16, 32, 128)

        @pl.loop(0, 8, unroll=8)
        def _(a):
            rhs = jnp.concatenate(
                [outer[2 * a].reshape(128, 128), outer[2 * a + 1].reshape(128, 128)], axis=1
            )
            u = jnp.dot(w2[c], rhs, preferred_element_type=F32)
            mid[2 * a] += u[:, :128]
            mid[2 * a + 1] += u[:, 128:]

    spread(0)
    spread_end(0)
    spread(1)
    spread_end(1)
    row_forward()

    for copy in later:
        copy.wait()
    s_tri[0:1024, :] = w_final[...].astype(F32)
    for d in range(32):
        part = s_tri[pl.ds(d, 32, stride=32), :]
        s_tri[1024 + d * 32 : 1024 + (d + 1) * 32, :] = part
    for b in range(8):
        w2[b] = s_tri[1024 + b * 128 : 1024 + (b + 1) * 128, :].T.astype(BF16)
    for b in range(4):
        t = w_six[b].astype(F32).T.astype(BF16)
        for g, n in enumerate(GROUPS):
            lo, n = 16 * sum(GROUPS[:g]), 16 * n
            w5[4 * lo + b * n : 4 * lo + (b + 1) * n, :] = t[lo : lo + n]
    for b in range(2):
        wu[b] = w_six[4 + b].astype(F32).T.astype(BF16)
    p_gain = column(gains[0])
    t_gain = column(gains[1])

    spread(2)
    forward(0)
    spread_end(2)

    remote(
        coup_h.at[:, other, :],
        coup16.at[pl.ds((1 - h) * 8, 8)],
        sib_send.at[1],
        sib_recv.at[1],
        sib,
    ).wait_recv()
    eye = (
        lax.broadcasted_iota(jnp.int32, (128, 128), 0)
        == lax.broadcasted_iota(jnp.int32, (128, 128), 1)
    ).astype(F32).astype(BF16)

    @pl.loop(0, 16, unroll=4)
    def _(i):
        mid[i] = lax.dot_general(eye, coup16[i], NT, preferred_element_type=F32)

    forward(1)
    remote(three, three, l_ssem.at[1], l_rsem.at[1], sib).wait_recv()
    l_fwd = remote(l_all.at[:, h], l_all.at[:, h], sib_send.at[2], sib_recv.at[2], sib)
    l_fwd.start()
    pending.append(l_fwd.wait_send)
    spread(3)
    spread_end(3)
    remote(
        l_all.at[:, 1 - h], l_all.at[:, 1 - h], sib_send.at[2], sib_recv.at[2], sib
    ).wait_recv()
    for b in range(4):
        l_t[b * 128 : (b + 1) * 128, :] = (
            l_all[:, :, :, b * 128 : (b + 1) * 128].reshape(512, 128).astype(F32).T.astype(BF16)
        )

    finish(0)
    row_forwarded()
    for c in range(4, LAST):
        spread(c)
        if c == 4:
            row_start()
        spread_end(c)
        forward(c - 2)
        finish(c - 3)
    row_relay()
    forward(LAST - 2)
    finish(LAST - 3)
    forward(LAST - 1)
    finish(LAST)
    finish(LAST - 2)
    finish(LAST - 1)


    zh = me // 16
    m_own = me % 16

    def e_near(g, m):
        return remote(
            e_send[g].at[m], e_recv[g].at[me], e_ssem, e_rsem.at[g], zh * 16 + m
        )

    def e_far(g, m):
        n = pl.ds(GROUPS[g], GROUPS[g])
        return remote(
            e_send[g].at[m, n],
            e_recv[g].at[me, n],
            e_ssem,
            e_rsem.at[g],
            (1 - zh) * 16 + m,
        )

    def edges(g, a):
        lo, n = 64 * sum(GROUPS[:g]), 16 * GROUPS[g]
        y = jnp.dot(w5[lo : lo + 4 * n], normed[a], preferred_element_type=F32)
        el = jax.nn.sigmoid(y[n : 2 * n]) * y[0:n]
        er = jax.nn.sigmoid(y[3 * n :]) * y[2 * n : 3 * n]
        for e in (0, 1):
            rows = pl.ds(2 * a + e, n, stride=16)
            s_el[rows, :] = el[:, e * 128 : (e + 1) * 128]
            s_er[rows, :] = er[:, e * 128 : (e + 1) * 128]

    def edges_send(g):
        n = GROUPS[g]

        @pl.loop(0, 16)
        def _(k):
            m = (m_own + k) % 16
            rows = pl.ds(pl.multiple_of(m * 16 * n, 16 * n), 16 * n)
            e_send[g][m, 0:n] = s_el[rows, :].reshape(n, 16, 128).astype(BF16)
            e_send[g][m, n : 2 * n] = s_er[rows, :].reshape(n, 16, 128).astype(BF16)
            e_far(g, m).start()

            @pl.when(k > 0)
            def _():
                e_near(g, m).start()

        e_recv[g][me] = e_send[g][m_own]

    @pl.loop(0, 8, unroll=2)
    def _(a):
        normed[a, :, 0:128] = norm_rows(mid[2 * a], p_gain)
        normed[a, :, 128:256] = norm_rows(mid[2 * a + 1], p_gain)
        edges(0, a)

    edges_send(0)

    for g in range(1, len(GROUPS)):
        pl.loop(0, 8, unroll=2)(functools.partial(edges, g))
        edges_send(g)
    sent(r_all.at[pl.ds(0, 23), pl.ds(0, 2)], e_ssem)

    @pl.loop(0, 8)
    def _(a):
        y = jax.nn.sigmoid(jnp.dot(wu[0], normed[a], preferred_element_type=F32))
        gate[2 * a] = y[:, :128]
        gate[2 * a + 1] = y[:, 128:]

    def t_copy(g, m):
        return remote(
            t_send[g].at[m // 2, m % 2],
            t_recv[g].at[m_own],
            t_ssem,
            t_rsem.at[g],
            zh * 16 + m,
        )

    for g, n in enumerate(GROUPS):
        every = r_all.at[pl.ds(0, 23), 0, pl.ds(0, 32 * n), :]
        remote(every, every, e_ssem, e_rsem.at[g], sib).wait_recv()

        got = e_recv[g].reshape(2, 8, 2, 2 * n, 16, 128)
        for c in range(n):
            t = None
            for hh in (0, 1):
                lhs = got[zh, :, hh, c].reshape(128, 128)
                rhs = got[:, :, hh, n + c].reshape(256, 128)
                term = lax.dot_general(lhs, rhs, NT, preferred_element_type=F32)
                t = term if t is None else t + term
            t = t.astype(BF16)
            for hh in (0, 1):
                t_send[g][:, hh, c] = t[:, hh * 128 : (hh + 1) * 128].reshape(8, 16, 128)

        @pl.loop(1, 16)
        def _(k):
            t_copy(g, (m_own + k) % 16).start()

        t_recv[g][m_own] = t_send[g][m_own // 2, h]

    sent(r_all.at[pl.ds(0, 15), 0], t_ssem)
    for g, n in enumerate(GROUPS):
        fifteen = t_recv[g].at[pl.ds(0, 15)]
        remote(fifteen, fifteen, t_ssem, t_rsem.at[g], sib).wait_recv()
        lo = 256 * sum(GROUPS[:g])
        s_tri[lo : lo + 256 * n, :] = t_recv[g][...].reshape(256 * n, 128).astype(F32)


    def result(a):
        rows = [
            norm_rows(s_tri[pl.ds(2 * a + e, 128, stride=16), :], t_gain) for e in (0, 1)
        ]
        y = jnp.dot(wu[1], jnp.concatenate(rows, axis=1), preferred_element_type=F32)
        for e in (0, 1):
            i = 2 * a + e
            r = mid[i] + gate[i] * y[:, e * 128 : (e + 1) * 128]
            o_buf[i] = r.T.astype(BF16)

    @pl.loop(0, 4, unroll=2)
    def _(a):
        result(4 * (1 - h) + a)

    o_copy = remote(
        o_buf.at[pl.ds((1 - h) * 8, 8)], o_got, sib_send.at[3], sib_recv.at[3], sib
    )
    o_copy.start()
    pending.append(o_copy.wait_send)

    @pl.loop(0, 4, unroll=2)
    def _(a):
        result(4 * h + a)

    out[:, mine, :] = o_buf[pl.ds(h * 8, 8)]
    o_copy.wait_recv()
    out[:, other, :] = o_got[...]

    for wait in pending:
        wait()


def local(
    relative_embedding,
    coupling_features,
    relative_variance_multiplier,
    bilinear_lhs_projector,
    bilinear_rhs_projector,
    product_final_matrix,
    coupling_standard_scale,
    incoming_edge_matrix,
    incoming_edge_sigmoid,
    second_edge_matrix,
    second_edge_sigmoid,
    update_sigmoid_matrix,
    update_final_matrix,
    cubic_standard_scale,
):
    vm = pltpu.VMEM
    dma = pltpu.SemaphoreType.DMA
    return pl.pallas_call(
        kernel,
        out_shape=jax.ShapeDtypeStruct((8, 256, 128), BF16),
        in_specs=[pl.BlockSpec(memory_space=pl.ANY)] * 14,
        out_specs=pl.BlockSpec(memory_space=pltpu.VMEM),
        scratch_shapes=[
            vm((16, 256, 256), BF16),
            vm((1, 256), F32),
            vm((32, 256), BF16),
            vm((32, 256), BF16),
            vm((1024, 128), BF16),
            vm((2, 1, 128), F32),
            vm((6, 128, 128), BF16),
            vm((4096, 128), F32),
            vm((2, 512, 128), F32),
            vm((16, 16, 512), BF16),
            vm((4, 4, 16, 512), BF16),
            vm((16, 2, 16, 512), BF16),
            vm((512, 512), BF16),
            vm((32, 16, 128), BF16),
            vm((32, 4, 128, 128), BF16),
            vm((16, ND, 32, 128), BF16),
            vm((16, 128, 128), BF16),
            vm((CHUNKS, 128, 128), BF16),
            vm((512, 128), BF16),
            vm((2, 128, 128), BF16),
            vm((16, 128, 128), F32),
            vm((16, 128, 128), F32),
            vm((8, 128, 256), BF16),
            vm((1024, 128), F32),
            vm((1024, 128), F32),
            [vm((16, 2 * n, 16, 128), BF16) for n in GROUPS],
            [vm((32, 2 * n, 16, 128), BF16) for n in GROUPS],
            [vm((8, 2, n, 16, 128), BF16) for n in GROUPS],
            [vm((16, n, 16, 128), BF16) for n in GROUPS],
            vm((2048, 128), F32),
            vm((16, 128, 128), BF16),
            vm((8, 128, 128), BF16),
            dma((12,)),
            dma((4,)),
            dma((4,)),
            dma((2,)),
            dma((2,)),
            dma,
            dma,
            dma,
            dma((CHUNKS,)),
            dma((CHUNKS,)),
            dma((CHUNKS, 2)),
            dma((CHUNKS, 2)),
            dma,
            dma((len(GROUPS),)),
            dma,
            dma((len(GROUPS),)),
        ],
        compiler_params=pltpu.CompilerParams(
            collective_id=0, has_side_effects=True, vmem_limit_bytes=60 * 1024 * 1024
        ),
    )(
        relative_embedding,
        coupling_features,
        relative_variance_multiplier.reshape(1, -1),
        bilinear_lhs_projector.T,
        bilinear_rhs_projector.T,
        product_final_matrix,
        coupling_standard_scale.reshape(1, -1),
        incoming_edge_matrix,
        incoming_edge_sigmoid,
        second_edge_matrix,
        second_edge_sigmoid,
        update_sigmoid_matrix,
        update_final_matrix,
        cubic_standard_scale.reshape(1, -1),
    )


def solution(mesh):
    rows = P(("batch", "dap"), None, None)
    return jax.shard_map(
        local,
        mesh=mesh,
        in_specs=(rows, rows) + (P(),) * 12,
        out_specs=rows,
        check_vma=False,
    )
```
